128 devices in a mesh: seq: 16 (over z, y), head: 8 (over x, core).
Axes of the slice: x: 4, y: 4, z: 4, core: 2. Of those that a mesh axis runs over, the one named last changes fastest.
Arguments:
- queries: bfloat16 [2048, 5120], P(None, 'head'), may hold values from -6 to 6
- doc_keys: bfloat16 [8192, 1024], P('seq', 'head'), may hold values from -6 to 6
- doc_values: bfloat16 [8192, 1024], P('seq', 'head'), may hold values from -6 to 6
- self_keys: bfloat16 [2048, 1024], P(None, 'head'), may hold values from -6 to 6
- self_values: bfloat16 [2048, 1024], P(None, 'head'), may hold values from -6 to 6
- out_grads: bfloat16 [2048, 5120], P(None, 'head'), may hold values from -96 to 96
- lengths: int32 [4], replicated, may hold values from 1 to 512, as said below
- query_weight: bfloat16 [5120, 5120], P('seq', 'head'), may hold values from -0.078125 to 0.078125
Outputs:
- input_grads: bfloat16 [2048, 5120], P('seq', 'head')
- doc_key_grads: float32 [8192, 1024], P('seq', 'head')
- doc_value_grads: float32 [8192, 1024], P('seq', 'head')
- self_key_grads: float32 [2048, 1024], P('seq', 'head')
- self_value_grads: float32 [2048, 1024], P('seq', 'head')
The draws below stay inside these ranges and needn't reach their ends.
Inputs may be any that keep to these rules, and one draw needn't show every extreme that they name: `lengths`: at least one response has all 512 tokens in every draw.
All inputs are finite; a program needn't handle non-finite values.
Results may differ from the reference program's by a relative error of at most 0.025.
Values may be sent and summed in bfloat16 or wider, within the bound.
No kernel may reach another device: no remote copies, remote signals or barrier semaphores. Data moves between devices by JAX's collectives and lax.ppermute only.
A program may use at most 128 MiB of HBM per device.

```python
import jax
import jax.numpy as jnp
from jax import lax

D = 5120
HQ = 40
KVH = 8
HD = 128
R = 4
L = 512
RT = 2048
DOC = 8192


def draw_queries(key, part):
    key = jax.random.fold_in(key, 1)
    values = jnp.clip(2.0 * jax.random.normal(key, (R * L, HQ * HD), jnp.float32), -6.0, 6.0)
    return values.astype(jnp.bfloat16)


def draw_doc_keys(key, part):
    key = jax.random.fold_in(key, 2)
    rising = 0.8 + 0.3 * jnp.arange(DOC, dtype=jnp.float32) / DOC
    values = jnp.clip(jax.random.normal(key, (DOC, KVH * HD), jnp.float32), -5.0, 5.0) * rising[:, None]
    return values.astype(jnp.bfloat16)


def draw_lengths(key, part):
    key = jax.random.fold_in(key, 3)
    first_key, second_key = jax.random.split(key)
    values = jax.random.permutation(first_key, L)[:R].astype(jnp.int32) + 1
    chosen = jax.random.randint(second_key, (), 0, R)
    return jnp.where(jnp.arange(R) == chosen, L, values).astype(jnp.int32)


def shard_levels(own_key, extent, shards, least, high):
    level = 1.0
    for axis_at, shards_of in shards:
        draws = jax.random.uniform(jax.random.fold_in(jax.random.fold_in(own_key, 6), axis_at), (shards_of,), jnp.float32, least / len(shards), high / len(shards))
        level = level * jnp.repeat(jnp.exp(draws), extent[axis_at] // shards_of).reshape((-1,) + (1,) * (len(extent) - 1 - axis_at))
    return level


def scatter_about(stream_key, extent, deviation, bound, cuts=(), kind=jnp.bfloat16):
    values = deviation * jax.random.normal(stream_key, extent, jnp.float32)
    if cuts:
        values = values * shard_levels(stream_key, extent, cuts, -0.22, 0.18)
    return jnp.clip(values, -bound, bound).astype(kind)


def setup_inputs(seed: int = 0) -> dict:
    streams_of = jax.random.split(jax.random.key(seed), 9)
    queries = draw_queries(jax.random.fold_in(streams_of[8], 71), 0)
    doc_keys = draw_doc_keys(jax.random.fold_in(streams_of[8], 71), 0)
    doc_values = scatter_about(streams_of[2], (DOC, KVH * HD), 1.0, 6.0, ((0, 16), (1, 8)))
    self_keys = scatter_about(streams_of[3], (RT, KVH * HD), 1.0, 6.0, ((1, 8),))
    self_values = scatter_about(streams_of[4], (RT, KVH * HD), 1.0, 6.0, ((1, 8),))
    out_grads = scatter_about(streams_of[5], (RT, HQ * HD), 16.0, 96.0, ((1, 8),))
    lengths = draw_lengths(jax.random.fold_in(streams_of[8], 71), 0)
    query_weight = scatter_about(streams_of[7], (D, HQ * HD), D ** -0.5, 0.078125, ((0, 16), (1, 8)))
    return dict(queries=queries, doc_keys=doc_keys, doc_values=doc_values, self_keys=self_keys, self_values=self_values, out_grads=out_grads, lengths=lengths, query_weight=query_weight)


def reference(queries, doc_keys, doc_values, self_keys, self_values, out_grads, lengths, query_weight):
    scale = HD ** -0.5
    head_group = HQ // KVH
    positions = jnp.arange(R * L, dtype=jnp.int32)
    owner = positions // L
    valid = (positions % L) < lengths[owner]
    masked = out_grads * valid[:, None].astype(out_grads.dtype)
    allowed = (owner[:, None] == owner[None, :]) & (positions[None, :] <= positions[:, None])
    q_heads = queries.reshape(R * L, KVH, head_group, HD).transpose(1, 2, 0, 3)
    g_heads = masked.reshape(R * L, KVH, head_group, HD).transpose(1, 2, 0, 3)

    def split_heads(array, count):
        return array.reshape(count, KVH, HD).transpose(1, 0, 2)

    def per_kv(items):
        q_group, g_group, doc_k, doc_v, self_k, self_v = items
        key_doc = jnp.zeros((DOC, HD), jnp.float32)
        value_doc = jnp.zeros((DOC, HD), jnp.float32)
        key_self = jnp.zeros((R * L, HD), jnp.float32)
        value_self = jnp.zeros((R * L, HD), jnp.float32)
        query_list = []
        for member in range(head_group):
            q_one = q_group[member]
            g_one = g_group[member]
            doc_s = scale * jnp.dot(q_one, doc_k.T, preferred_element_type=jnp.float32)
            self_s = jnp.where(allowed, scale * jnp.dot(q_one, self_k.T, preferred_element_type=jnp.float32), -jnp.inf)
            top = jnp.maximum(jnp.max(doc_s, axis=1), jnp.max(self_s, axis=1))
            total = jnp.sum(jnp.exp(doc_s - top[:, None]), axis=1) + jnp.sum(jnp.exp(self_s - top[:, None]), axis=1)
            log_sum = top + jnp.log(total)
            doc_p = jnp.exp(doc_s - log_sum[:, None])
            self_p = jnp.where(allowed, jnp.exp(self_s - log_sum[:, None]), 0.0)
            doc_dp = jnp.dot(g_one, doc_v.T, preferred_element_type=jnp.float32)
            self_dp = jnp.dot(g_one, self_v.T, preferred_element_type=jnp.float32)
            delta = jnp.sum(doc_p * doc_dp, axis=1) + jnp.sum(self_p * self_dp, axis=1)
            doc_ds = (doc_p * (doc_dp - delta[:, None])).astype(jnp.bfloat16)
            self_ds = (self_p * (self_dp - delta[:, None])).astype(jnp.bfloat16)
            query_list.append(scale * (jnp.dot(doc_ds, doc_k, preferred_element_type=jnp.float32)
                                       + jnp.dot(self_ds, self_k, preferred_element_type=jnp.float32)))
            key_doc = key_doc + scale * jnp.dot(doc_ds.T, q_one, preferred_element_type=jnp.float32)
            value_doc = value_doc + jnp.dot(doc_p.astype(jnp.bfloat16).T, g_one, preferred_element_type=jnp.float32)
            key_self = key_self + scale * jnp.dot(self_ds.T, q_one, preferred_element_type=jnp.float32)
            value_self = value_self + jnp.dot(self_p.astype(jnp.bfloat16).T, g_one, preferred_element_type=jnp.float32)
        return jnp.stack(query_list), key_doc, value_doc, key_self, value_self

    query_all, key_doc, value_doc, key_self, value_self = lax.map(
        per_kv, (q_heads, g_heads, split_heads(doc_keys, DOC), split_heads(doc_values, DOC),
                 split_heads(self_keys, R * L), split_heads(self_values, R * L)))
    query_grads = query_all.transpose(2, 0, 1, 3).reshape(R * L, HQ * HD).astype(jnp.bfloat16)
    input_grads = jnp.dot(query_grads, query_weight.T, preferred_element_type=jnp.float32).astype(jnp.bfloat16)

    def join_heads(array):
        return array.transpose(1, 0, 2).reshape(array.shape[1], KVH * HD)

    return input_grads, join_heads(key_doc), join_heads(value_doc), join_heads(key_self), join_heads(value_self)
```

```python
import math

import jax
import jax.numpy as jnp
from jax import lax
from jax.experimental import pallas as pl
from jax.experimental.pallas import tpu as pltpu
from jax.sharding import PartitionSpec as P

HQ = 40
KVH = 8
HD = 128
L = 512
GROUP = HQ // KVH
FACTOR = HD ** (-0.5)
LOG_FACTOR = FACTOR * math.log2(math.e)
STATS = 16
BF16 = jnp.bfloat16
F32 = jnp.float32


def dot_nt(a, b):
    return lax.dot_general(a, b, (((1,), (1,)), ((), ())), preferred_element_type=F32)


def dot_nn(a, b):
    return lax.dot_general(a, b, (((1,), (0,)), ((), ())), preferred_element_type=F32)


def keep_valid(grads, length, start):
    rows = lax.broadcasted_iota(jnp.int32, grads.shape, 0) + start
    return jnp.where(rows < length, grads, jnp.zeros_like(grads))


def local_stats(scores, dprods):
    top = jnp.max(scores, axis=0, keepdims=True)
    weights = jnp.exp2(scores - top)
    total = jnp.sum(weights, axis=0, keepdims=True)
    mixed = jnp.sum(weights * dprods, axis=0, keepdims=True)
    return top, total, mixed


def stats_kernel(info, q_ref, g_ref, k_ref, v_ref, sk_ref, sv_ref, out_ref, own_ref):
    head = pl.program_id(0)
    slot = info[0]

    @pl.when(head == 0)
    def _():
        out_ref[...] = jnp.zeros_like(out_ref)
        own_ref[...] = jnp.zeros_like(own_ref)

    for block in range(q_ref.shape[0] // L):
        q = q_ref[block * L : (block + 1) * L, :]
        g = keep_valid(g_ref[block * L : (block + 1) * L, :], info[1 + block], 0)
        found = local_stats(dot_nt(k_ref[...], q) * LOG_FACTOR, dot_nt(v_ref[...], g))
        for part in range(L // HD):
            for kind in range(3):
                out_ref[block * (L // HD) + part, pl.ds(kind * GROUP + head, 1), :] = found[kind][
                    :, part * HD : (part + 1) * HD
                ]
    start = lax.rem(slot, L // HD) * HD
    q = q_ref[pl.ds(slot * HD, HD), :]
    g = keep_valid(g_ref[pl.ds(slot * HD, HD), :], info[1 + lax.div(slot, L // HD)], start)
    scores = dot_nt(sk_ref[...], q) * LOG_FACTOR
    keys = lax.broadcasted_iota(jnp.int32, scores.shape, 0)
    rows = lax.broadcasted_iota(jnp.int32, scores.shape, 1) + start
    found = local_stats(jnp.where(keys <= rows, scores, -jnp.inf), dot_nt(sv_ref[...], g))
    for kind in range(3):
        own_ref[pl.ds(kind * GROUP + head, 1), :] = found[kind]


def combine_kernel(parts_ref, own_ref, out_ref):
    parts = parts_ref[...]
    own = own_ref[...]
    top = jnp.maximum(jnp.max(parts[:, :GROUP], axis=0), own[:GROUP])
    own_scale = jnp.exp2(own[:GROUP] - top)
    scale = jnp.exp2(parts[:, :GROUP] - top[None])
    total = own[GROUP : 2 * GROUP] * own_scale + jnp.sum(parts[:, GROUP : 2 * GROUP] * scale, axis=0)
    mixed = own[2 * GROUP : 3 * GROUP] * own_scale + jnp.sum(
        parts[:, 2 * GROUP : 3 * GROUP] * scale, axis=0
    )
    log_sum = top + jnp.log2(total)
    delta = mixed / total
    rest = jnp.zeros((STATS - 2 * GROUP, HD), F32)
    final = jnp.concatenate([log_sum, delta, rest], axis=0)
    out_ref[...] = jnp.broadcast_to(final[None], out_ref.shape)


def score_grads(k, v, q, g, log_sum, delta, allowed=None):
    probs = jnp.exp2(dot_nt(k, q) * LOG_FACTOR - log_sum)
    if allowed is not None:
        probs = jnp.where(allowed, probs, 0.0)
    dscores = (probs * (dot_nt(v, g) - delta)).astype(BF16)
    return probs.astype(BF16), dscores


def grads_kernel(
    info, q_ref, g_ref, k_ref, v_ref, sk_ref, sv_ref, ok_ref, ov_ref, stat_ref,
    dq_ref, dk_ref, dv_ref, dqs_ref, dsk_ref, dsv_ref, kt_ref, skt_ref,
):
    head = pl.program_id(0)
    slot = info[0]
    per = L // HD

    @pl.when(head == 0)
    def _():
        dk_ref[...] = jnp.zeros_like(dk_ref)
        dv_ref[...] = jnp.zeros_like(dv_ref)
        dsk_ref[...] = jnp.zeros_like(dsk_ref)
        dsv_ref[...] = jnp.zeros_like(dsv_ref)
        kt_ref[...] = k_ref[...].T
        skt_ref[...] = sk_ref[...].T

    def row_stats(first, count, offset):
        return jnp.concatenate(
            [stat_ref[first + i, pl.ds(offset + head, 1), :] for i in range(count)], axis=1
        )

    dk = jnp.zeros(dk_ref.shape, F32)
    dv = jnp.zeros(dv_ref.shape, F32)
    for block in range(q_ref.shape[0] // L):
        q = q_ref[block * L : (block + 1) * L, :]
        g = keep_valid(g_ref[block * L : (block + 1) * L, :], info[1 + block], 0)
        log_sum = row_stats(block * per, per, 0)
        delta = row_stats(block * per, per, GROUP)
        probs, dscores = score_grads(k_ref[...], v_ref[...], q, g, log_sum, delta)
        dv = dv + dot_nn(probs, g)
        dk = dk + dot_nn(dscores, q)
        dq = dot_nn(kt_ref[...], dscores) * FACTOR
        dq_ref[block * L : (block + 1) * L, :] = dq.T.astype(BF16)
    dk_ref[...] += dk * FACTOR
    dv_ref[...] += dv

    response = lax.div(slot, per)
    start = lax.rem(slot, per) * HD
    q = q_ref[pl.ds(slot * HD, HD), :]
    g = keep_valid(g_ref[pl.ds(slot * HD, HD), :], info[1 + response], start)
    keys = lax.broadcasted_iota(jnp.int32, (L, HD), 0)
    rows = lax.broadcasted_iota(jnp.int32, (L, HD), 1) + start
    _, dscores = score_grads(
        sk_ref[...], sv_ref[...], q, g, row_stats(slot, 1, 0), row_stats(slot, 1, GROUP), keys <= rows
    )
    dqs_ref[...] = (dot_nn(skt_ref[...], dscores) * FACTOR).T

    q = q_ref[pl.ds(response * L, L), :]
    g = keep_valid(g_ref[pl.ds(response * L, L), :], info[1 + response], 0)
    keys = lax.broadcasted_iota(jnp.int32, (HD, L), 0) + start
    rows = lax.broadcasted_iota(jnp.int32, (HD, L), 1)
    first = response * per
    probs, dscores = score_grads(
        ok_ref[...], ov_ref[...], q, g, row_stats(first, per, 0), row_stats(first, per, GROUP), keys <= rows
    )
    dsk_ref[...] += dot_nn(dscores, q) * FACTOR
    dsv_ref[...] += dot_nn(probs, g)


def project_kernel(parts_ref, own_ref, w_ref, out_ref, dq_ref):
    @pl.when(pl.program_id(0) == 0)
    def _():
        total = own_ref[...]
        for part in range(parts_ref.shape[0]):
            total = total + parts_ref[part].astype(F32)
        dq_ref[...] = total.astype(BF16)

    out_ref[...] = dot_nt(dq_ref[...], w_ref[...])[None].astype(BF16)


def sum_kernel(parts_ref, out_ref):
    total = parts_ref[0].astype(F32)
    for part in range(1, parts_ref.shape[0]):
        total = total + parts_ref[part].astype(F32)
    out_ref[...] = total.astype(BF16)


def params(megabytes=48):
    return pltpu.CompilerParams(
        dimension_semantics=("arbitrary",), vmem_limit_bytes=megabytes * 1024 * 1024
    )


def body(queries, doc_keys, doc_values, self_keys, self_values, out_grads, lengths, query_weight):
    rows_all = queries.shape[0]
    doc_rows = doc_keys.shape[0]
    shards = lax.axis_size("seq")
    groups = lax.axis_size("head")
    own_rows = rows_all // shards
    per = L // own_rows
    slot = lax.axis_index("seq").astype(jnp.int32)
    info = jnp.concatenate([slot[None], lengths.astype(jnp.int32)])
    weight = lax.all_gather(query_weight, "seq", axis=0, tiled=True)

    rows_spec = pl.BlockSpec((rows_all, HD), lambda h, info: (0, h))
    doc_spec = pl.BlockSpec((doc_rows, HD), lambda h, info: (0, 0))
    response_spec = pl.BlockSpec((L, HD), lambda h, info: (info[0] // per, 0))
    own_spec = pl.BlockSpec((own_rows, HD), lambda h, info: (info[0], 0))
    stat_spec = pl.BlockSpec((shards, STATS, HD), lambda h, info: (0, 0, 0))

    stats, own_stats = pl.pallas_call(
        stats_kernel,
        grid_spec=pltpu.PrefetchScalarGridSpec(
            num_scalar_prefetch=1,
            grid=(GROUP,),
            in_specs=[rows_spec, rows_spec, doc_spec, doc_spec, response_spec, response_spec],
            out_specs=[stat_spec, pl.BlockSpec((STATS, HD), lambda h, info: (0, 0))],
        ),
        out_shape=[
            jax.ShapeDtypeStruct((shards, STATS, HD), F32),
            jax.ShapeDtypeStruct((STATS, HD), F32),
        ],
        compiler_params=params(),
        name="local_stats",
    )(info, queries, out_grads, doc_keys, doc_values, self_keys, self_values)
    parts = lax.all_to_all(stats, "seq", 0, 0, tiled=True)
    final = pl.pallas_call(
        combine_kernel,
        out_shape=jax.ShapeDtypeStruct((shards, STATS, HD), F32),
        name="combine_stats",
    )(parts, own_stats)
    final = lax.all_to_all(final, "seq", 0, 0, tiled=True)

    dq, dk, dv, dqs, dsk, dsv = pl.pallas_call(
        grads_kernel,
        grid_spec=pltpu.PrefetchScalarGridSpec(
            num_scalar_prefetch=1,
            grid=(GROUP,),
            in_specs=[
                rows_spec, rows_spec, doc_spec, doc_spec, response_spec, response_spec,
                own_spec, own_spec, stat_spec,
            ],
            out_specs=[
                rows_spec, doc_spec, doc_spec,
                pl.BlockSpec((own_rows, HD), lambda h, info: (0, h)),
                pl.BlockSpec((own_rows, HD), lambda h, info: (0, 0)),
                pl.BlockSpec((own_rows, HD), lambda h, info: (0, 0)),
            ],
            scratch_shapes=[pltpu.VMEM((HD, doc_rows), BF16), pltpu.VMEM((HD, L), BF16)],
        ),
        out_shape=[
            jax.ShapeDtypeStruct((rows_all, GROUP * HD), BF16),
            jax.ShapeDtypeStruct((doc_rows, HD), F32),
            jax.ShapeDtypeStruct((doc_rows, HD), F32),
            jax.ShapeDtypeStruct((own_rows, GROUP * HD), F32),
            jax.ShapeDtypeStruct((own_rows, HD), F32),
            jax.ShapeDtypeStruct((own_rows, HD), F32),
        ],
        compiler_params=params(),
        name="local_grads",
    )(
        info, queries, out_grads, doc_keys, doc_values, self_keys, self_values,
        self_keys, self_values, final,
    )
    width = GROUP * HD
    dq_parts = lax.all_to_all(dq.reshape(shards, own_rows, width), "seq", 0, 0, tiled=True)
    terms = pl.pallas_call(
        project_kernel,
        grid=(groups,),
        in_specs=[
            pl.BlockSpec((shards, own_rows, width), lambda i: (0, 0, 0)),
            pl.BlockSpec((own_rows, width), lambda i: (0, 0)),
            pl.BlockSpec((weight.shape[0] // groups, width), lambda i: (i, 0)),
        ],
        out_specs=pl.BlockSpec((1, own_rows, weight.shape[0] // groups), lambda i: (i, 0, 0)),
        out_shape=jax.ShapeDtypeStruct((groups, own_rows, weight.shape[0] // groups), BF16),
        scratch_shapes=[pltpu.VMEM((own_rows, width), BF16)],
        compiler_params=params(),
        name="project",
    )(dq_parts, dqs, weight)
    terms = lax.all_to_all(terms, "head", 0, 0, tiled=True)
    input_grads = pl.pallas_call(
        sum_kernel,
        out_shape=jax.ShapeDtypeStruct(terms.shape[1:], BF16),
        name="sum_groups",
    )(terms)
    return input_grads, dk, dv, dsk, dsv


def solution(mesh):
    in_specs = (
        P(None, "head"),
        P("seq", "head"),
        P("seq", "head"),
        P(None, "head"),
        P(None, "head"),
        P(None, "head"),
        P(),
        P("seq", "head"),
    )
    out_specs = (
        P("seq", "head"),
        P("seq", "head"),
        P("seq", "head"),
        P("seq", "head"),
        P("seq", "head"),
    )
    return jax.shard_map(body, mesh=mesh, in_specs=in_specs, out_specs=out_specs, check_vma=False)
```

```python
import functools
import math

import jax
import jax.numpy as jnp
from jax import lax
from jax.experimental import pallas as pl
from jax.experimental.pallas import tpu as pltpu
from jax.sharding import Mesh, PartitionSpec as P

HQ = 40
KVH = 8
HD = 128
L = 512
GROUP = HQ // KVH
WIDTH = GROUP * HD
FACTOR = HD ** (-0.5)
LOG_FACTOR = FACTOR * math.log2(math.e)
STATS = 16
SIDE = 4
LOW = -1e30
BF16 = jnp.bfloat16
F32 = jnp.float32


def dot_nt(a, b):
    return lax.dot_general(a, b, (((1,), (1,)), ((), ())), preferred_element_type=F32)


def dot_nn(a, b):
    return lax.dot_general(a, b, (((1,), (0,)), ((), ())), preferred_element_type=F32)


def load_rows(ref):
    return ref[...].reshape(SIDE * HD, HD)


def load_valid(ref, info):
    pieces = []
    for response in range(SIDE):
        piece = ref[response]
        rows = lax.broadcasted_iota(jnp.int32, piece.shape, 0) + info[1] * HD
        pieces.append(jnp.where(rows < info[2 + response], piece, jnp.zeros_like(piece)))
    return jnp.concatenate(pieces, axis=0)


def load_own(ref, info, masked):
    piece = ref[info[0]]
    if not masked:
        return piece
    rows = lax.broadcasted_iota(jnp.int32, piece.shape, 0) + info[1] * HD
    return jnp.where(rows < info[2 + info[0]], piece, jnp.zeros_like(piece))


def own_lanes(row, info):
    pieces = [row[:, i * HD : (i + 1) * HD] for i in range(SIDE)]
    return sum(jnp.where(info[0] == i, piece, 0.0) for i, piece in enumerate(pieces))


def causal(info):
    keys = lax.broadcasted_iota(jnp.int32, (L, HD), 0)
    rows = lax.broadcasted_iota(jnp.int32, (L, HD), 1) + info[1] * HD
    return keys <= rows


def local_stats(scores, dprods):
    top = jnp.max(scores, axis=0, keepdims=True)
    weights = jnp.exp2(scores - top)
    total = jnp.sum(weights, axis=0, keepdims=True)
    mixed = jnp.sum(weights * dprods, axis=0, keepdims=True)
    return top, total, mixed


def merge(found):
    top = functools.reduce(jnp.maximum, [item[0] for item in found])
    scales = [jnp.exp2(item[0] - top) for item in found]
    total = sum(item[1] * scale for item, scale in zip(found, scales))
    mixed = sum(item[2] * scale for item, scale in zip(found, scales))
    return top, total, mixed


def stats_kernel(chunks, with_self, with_former, info, *refs):
    refs = list(refs)
    q_ref, g_ref = refs[:2]
    key_refs = refs[2 : 2 + chunks]
    value_refs = refs[2 + chunks : 2 + 2 * chunks]
    rest = refs[2 + 2 * chunks :]
    out_ref = rest[-1]
    head = pl.program_id(0)

    @pl.when(head == 0)
    def _():
        out_ref[...] = jnp.zeros_like(out_ref)

    q = load_rows(q_ref)
    g = load_valid(g_ref, info)
    found = [
        local_stats(dot_nt(k[...], q) * LOG_FACTOR, dot_nt(v[...], g))
        for k, v in zip(key_refs, value_refs)
    ]
    if with_self:
        q = load_own(q_ref, info, False)
        g = load_own(g_ref, info, True)
        scores = jnp.where(causal(info), dot_nt(rest[0][...], q) * LOG_FACTOR, -jnp.inf)
        own = local_stats(scores, dot_nt(rest[1][...], g))
        mine = lax.broadcasted_iota(jnp.int32, (1, SIDE * HD), 1) // HD == info[0]
        found.append(
            tuple(
                jnp.where(mine, jnp.concatenate([item] * SIDE, axis=1), other)
                for item, other in zip(own, (LOW, 0.0, 0.0))
            )
        )
    if with_former:
        found.append(tuple(rest[0][pl.ds(kind * GROUP + head, 1), :] for kind in range(3)))
    found = merge(found) if len(found) > 1 else found[0]
    for kind in range(3):
        out_ref[pl.ds(kind * GROUP + head, 1), :] = found[kind]


def score_grads(k, v, q, g, log_sum, delta, allowed=None):
    probs = jnp.exp2(dot_nt(k, q) * LOG_FACTOR - log_sum)
    if allowed is not None:
        probs = jnp.where(allowed, probs, 0.0)
    dscores = (probs * (dot_nt(v, g) - delta)).astype(BF16)
    return probs.astype(BF16), dscores


def grads_kernel(info, *refs):
    q_ref, g_ref = refs[:2]
    key_refs = refs[2:6]
    value_refs = refs[6:10]
    sk_ref, sv_ref = refs[10:12]
    part_refs = refs[12:16]
    dq_ref, dk_ref, dv_ref, dsk_ref, dsv_ref = refs[16:21]
    send_refs = refs[21:24]
    stat_ref, keyt_ref, skt_ref, dkey_ref, dvalue_ref, dself_key_ref, dself_value_ref = refs[24:]
    head = pl.program_id(0)

    @pl.when(head == 0)
    def _():
        parts = [
            tuple(ref[kind * GROUP : (kind + 1) * GROUP, :] for kind in range(3)) for ref in part_refs
        ]
        top, total, mixed = merge(parts)
        stat_ref[:GROUP, :] = top + jnp.log2(total)
        stat_ref[GROUP : 2 * GROUP, :] = mixed / total
        for i in range(SIDE):
            keyt_ref[i] = key_refs[i][...].T
        skt_ref[...] = sk_ref[...].T
        dkey_ref[...] = jnp.zeros_like(dkey_ref)
        dvalue_ref[...] = jnp.zeros_like(dvalue_ref)
        dself_key_ref[...] = jnp.zeros_like(dself_key_ref)
        dself_value_ref[...] = jnp.zeros_like(dself_value_ref)

    log_sum = stat_ref[pl.ds(head, 1), :]
    delta = stat_ref[pl.ds(GROUP + head, 1), :]
    q = load_rows(q_ref)
    g = load_valid(g_ref, info)
    dq = jnp.zeros((HD, SIDE * HD), F32)
    for i in range(SIDE):
        probs, dscores = score_grads(key_refs[i][...], value_refs[i][...], q, g, log_sum, delta)
        dvalue_ref[i] += dot_nn(probs, g)
        dkey_ref[i] += dot_nn(dscores, q)
        dq = dq + dot_nn(keyt_ref[i], dscores)

    q = load_own(q_ref, info, False)
    g = load_own(g_ref, info, True)
    probs, dscores = score_grads(
        sk_ref[...], sv_ref[...], q, g, own_lanes(log_sum, info), own_lanes(delta, info), causal(info)
    )
    dself_value_ref[...] += dot_nn(probs, g)
    dself_key_ref[...] += dot_nn(dscores, q)
    own = dot_nn(skt_ref[...], dscores)
    for response in range(SIDE):
        piece = dq[:, response * HD : (response + 1) * HD]
        piece = piece + jnp.where(response == info[0], own, 0.0)
        dq_ref[response] = (piece * FACTOR).T.astype(BF16)

    @pl.when(head == GROUP - 1)
    def _():
        def self_rows(place):
            return pl.ds(pl.multiple_of(lax.rem(info[1] + place, SIDE) * HD, HD), HD)

        dk_ref[...] = dkey_ref[0] * FACTOR
        dv_ref[...] = dvalue_ref[0]
        dsk_ref[...] = dself_key_ref[self_rows(0), :] * FACTOR
        dsv_ref[...] = dself_value_ref[self_rows(0), :]
        for send_ref, i, place in zip(send_refs, (1, 2, 3), (3, 1, 2)):
            send_ref[:L, :HD] = (dkey_ref[i] * FACTOR).astype(BF16)
            send_ref[:L, HD:] = dvalue_ref[i].astype(BF16)
            send_ref[L:, :HD] = (dself_key_ref[self_rows(place), :] * FACTOR).astype(BF16)
            send_ref[L:, HD:] = dself_value_ref[self_rows(place), :].astype(BF16)


def finish_kernel(dk_ref, dv_ref, dsk_ref, dsv_ref, a_ref, b_ref, c_ref, dk_out, dv_out, dsk_out, dsv_out):
    def total(own_ref, rows, columns):
        return own_ref[...] + sum(ref[rows, columns].astype(F32) for ref in (a_ref, b_ref, c_ref))

    doc, slots = slice(0, L), slice(L, L + HD)
    keys, values = slice(0, HD), slice(HD, 2 * HD)
    dk_out[...] = total(dk_ref, doc, keys)
    dv_out[...] = total(dv_ref, doc, values)
    dsk_out[...] = total(dsk_ref, slots, keys)
    dsv_out[...] = total(dsv_ref, slots, values)


def sum_kernel(parts_ref, out_ref):
    total = parts_ref[0].astype(F32)
    for part in range(1, parts_ref.shape[0]):
        total = total + parts_ref[part].astype(F32)
    out_ref[...] = total.astype(BF16)


def sum_turn_kernel(parts_ref, out_ref):
    total = parts_ref[0].astype(F32)
    for part in range(1, parts_ref.shape[0]):
        total = total + parts_ref[part].astype(F32)
    out_ref[...] = total.T.astype(BF16)


def project_kernel(info, *refs):
    grad_refs = refs[:4]
    weight_refs = refs[4:8]
    mine_ref, theirs_ref = refs[8:10]
    rows_ref = refs[10]
    for i, place in enumerate((0, 3, 1, 2)):
        at = pl.multiple_of(lax.rem(info[0] + place, SIDE) * HD, HD)
        rows_ref[pl.ds(at, HD), :] = grad_refs[i][...]
    depth = weight_refs[0].shape[0]
    for i, place in enumerate((0, 3, 1, 2)):
        block = lax.rem(info[1] + place, SIDE)
        terms = dot_nt(weight_refs[i][...], rows_ref[...]).astype(BF16)
        at = pl.ds(pl.multiple_of(lax.rem(block, 2) * depth, depth), depth)
        same = lax.div(block, 2) == info[2 + SIDE]

        @pl.when(same)
        def _():
            for response in range(SIDE):
                mine_ref[response, at, :] = terms[:, response * HD : (response + 1) * HD]

        @pl.when(jnp.logical_not(same))
        def _():
            for response in range(SIDE):
                theirs_ref[response, at, :] = terms[:, response * HD : (response + 1) * HD]


def params(megabytes=56):
    return pltpu.CompilerParams(vmem_limit_bytes=megabytes * 1024 * 1024)


def ring(step):
    return [(i, (i + step) % SIDE) for i in range(SIDE)]


def spread(array, axis):
    return [lax.ppermute(array, axis, ring(step)) for step in (1, 3, 2)]


def body(queries, doc_keys, doc_values, self_keys, self_values, out_grads, lengths, query_weight):
    doc_rows = doc_keys.shape[0]
    info = jnp.concatenate(
        [
            lax.axis_index("z").astype(jnp.int32)[None],
            lax.axis_index("y").astype(jnp.int32)[None],
            lengths.astype(jnp.int32),
            lax.axis_index("core").astype(jnp.int32)[None],
        ]
    )
    q_four = queries.reshape(SIDE, L, WIDTH)
    g_four = out_grads.reshape(SIDE, L, WIDTH)

    keys_low, values_low = (lax.ppermute(a, "y", ring(1)) for a in (doc_keys, doc_values))
    keys_high, values_high = (lax.ppermute(a, "y", ring(3)) for a in (doc_keys, doc_values))
    keys_far = lax.ppermute(keys_low, "y", ring(1))
    values_far = lax.ppermute(values_high, "y", ring(3))
    weight, _ = lax.optimization_barrier((query_weight, keys_low))
    weights = [query_weight] + spread(weight, "y")

    rows_spec = pl.BlockSpec((SIDE, HD, HD), lambda h, info: (0, info[1], h))
    doc_spec = pl.BlockSpec((doc_rows, HD), lambda h, info: (0, 0))
    response_spec = pl.BlockSpec((L, HD), lambda h, info: (info[0], 0))
    stat_spec = pl.BlockSpec((STATS, SIDE * HD), lambda h, info: (0, 0))
    stat_shape = jax.ShapeDtypeStruct((STATS, SIDE * HD), F32)

    def stats_call(keys, values, own=(), former=()):
        chunks = len(keys)
        elements = chunks * GROUP * SIDE * HD * doc_rows
        return pl.pallas_call(
            functools.partial(stats_kernel, chunks, bool(own), bool(former)),
            grid_spec=pltpu.PrefetchScalarGridSpec(
                num_scalar_prefetch=1,
                grid=(GROUP,),
                in_specs=[rows_spec] * 2
                + [doc_spec] * (2 * chunks)
                + [response_spec] * len(own)
                + [stat_spec] * len(former),
                out_specs=stat_spec,
            ),
            out_shape=stat_shape,
            compiler_params=params(),
            cost_estimate=pl.CostEstimate(
                flops=4 * elements * HD, bytes_accessed=2**21, transcendentals=elements
            ),
            name="local_stats",
        )(info, q_four, g_four, *keys, *values, *own, *former)

    stats = stats_call([doc_keys], [doc_values], own=(self_keys, self_values))
    stats = stats_call([keys_low, keys_high], [values_low, values_high], former=(stats,))
    stats = stats_call([keys_far], [values_far], former=(stats,))
    parts = [stats] + spread(stats, "z")

    elements = GROUP * SIDE * HD * doc_rows * SIDE
    dq, dk, dv, dsk, dsv, *sends = pl.pallas_call(
        grads_kernel,
        grid_spec=pltpu.PrefetchScalarGridSpec(
            num_scalar_prefetch=1,
            grid=(GROUP,),
            in_specs=[rows_spec] * 2 + [doc_spec] * 8 + [response_spec] * 2 + [stat_spec] * 4,
            out_specs=[pl.BlockSpec((SIDE, HD, HD), lambda h, info: (0, 0, h))]
            + [doc_spec] * 2
            + [pl.BlockSpec((HD, HD), lambda h, info: (0, 0))] * 2
            + [pl.BlockSpec((doc_rows + HD, 2 * HD), lambda h, info: (0, 0))] * 3,
            scratch_shapes=[
                pltpu.VMEM((STATS, SIDE * HD), F32),
                pltpu.VMEM((SIDE, HD, doc_rows), BF16),
                pltpu.VMEM((HD, L), BF16),
                pltpu.VMEM((SIDE, doc_rows, HD), F32),
                pltpu.VMEM((SIDE, doc_rows, HD), F32),
                pltpu.VMEM((L, HD), F32),
                pltpu.VMEM((L, HD), F32),
            ],
        ),
        out_shape=[jax.ShapeDtypeStruct((SIDE, HD, WIDTH), BF16)]
        + [jax.ShapeDtypeStruct((doc_rows, HD), F32)] * 2
        + [jax.ShapeDtypeStruct((HD, HD), F32)] * 2
        + [jax.ShapeDtypeStruct((doc_rows + HD, 2 * HD), BF16)] * 3,
        compiler_params=params(),
        cost_estimate=pl.CostEstimate(
            flops=10 * elements * HD, bytes_accessed=2**23, transcendentals=elements
        ),
        name="local_grads",
    )(
        info, q_four, g_four, doc_keys, keys_low, keys_high, keys_far,
        doc_values, values_low, values_high, values_far, self_keys, self_values, *parts,
    )
    backs = [lax.ppermute(a, "y", ring(step)) for a, step in zip(sends, (3, 1, 2))]

    dq_parts = lax.all_to_all(dq, "z", 0, 0, tiled=True)
    dq = pl.pallas_call(
        sum_kernel,
        out_shape=jax.ShapeDtypeStruct((HD, WIDTH), BF16),
        name="sum_shards",
    )(dq_parts)
    grads = [dq] + spread(dq, "z")
    columns = 2 * query_weight.shape[0]
    mine, theirs = pl.pallas_call(
        project_kernel,
        in_specs=[pl.BlockSpec(memory_space=pltpu.SMEM)]
        + [pl.BlockSpec(memory_space=pltpu.VMEM)] * 8,
        out_shape=[jax.ShapeDtypeStruct((SIDE, columns, HD), BF16)] * 2,
        scratch_shapes=[pltpu.VMEM((SIDE * HD, WIDTH), BF16)],
        compiler_params=params(32),
        name="project",
    )(info, *grads, *weights)
    theirs = lax.ppermute(theirs, "core", [(0, 1), (1, 0)])
    terms = (mine.astype(F32) + theirs.astype(F32)).astype(BF16)
    terms = lax.all_to_all(terms, "z", 0, 0, tiled=True)
    terms = lax.all_to_all(terms, "x", 0, 0, tiled=True)
    input_grads = pl.pallas_call(
        sum_turn_kernel,
        out_shape=jax.ShapeDtypeStruct((HD, columns), BF16),
        name="sum_groups",
    )(terms)
    dk, dv, dsk, dsv = pl.pallas_call(
        finish_kernel,
        out_shape=[jax.ShapeDtypeStruct((doc_rows, HD), F32)] * 2
        + [jax.ShapeDtypeStruct((HD, HD), F32)] * 2,
        name="sum_key_values",
    )(dk, dv, dsk, dsv, *backs)
    return input_grads, dk, dv, dsk, dsv


def solution(mesh):
    grid = Mesh(mesh.devices.reshape(SIDE, SIDE, SIDE, 2), ("z", "y", "x", "core"))
    seq, head = ("z", "y"), ("x", "core")
    in_specs = (
        P(None, head),
        P(seq, head),
        P(seq, head),
        P(None, head),
        P(None, head),
        P(None, head),
        P(),
        P(seq, head),
    )
    return jax.shard_map(
        body, mesh=grid, in_specs=in_specs, out_specs=(P(seq, head),) * 5, check_vma=False
    )
```

```python
import functools
import math

import jax
import jax.numpy as jnp
from jax import lax
from jax.experimental import pallas as pl
from jax.experimental.pallas import tpu as pltpu
from jax.sharding import Mesh, PartitionSpec as P

HQ = 40
KVH = 8
HD = 128
L = 512
GROUP = HQ // KVH
WIDTH = GROUP * HD
FACTOR = HD ** (-0.5)
LOG_FACTOR = FACTOR * math.log2(math.e)
STATS = 16
SIDE = 4
LOW = -1e30
BF16 = jnp.bfloat16
F32 = jnp.float32


def dot_nt(a, b):
    return lax.dot_general(a, b, (((1,), (1,)), ((), ())), preferred_element_type=F32)


def dot_nn(a, b):
    return lax.dot_general(a, b, (((1,), (0,)), ((), ())), preferred_element_type=F32)


def load_rows(ref):
    return ref[...].reshape(SIDE * HD, HD)


def load_valid(ref, info):
    pieces = []
    for response in range(SIDE):
        piece = ref[response]
        rows = lax.broadcasted_iota(jnp.int32, piece.shape, 0) + info[1] * HD
        pieces.append(jnp.where(rows < info[2 + response], piece, jnp.zeros_like(piece)))
    return jnp.concatenate(pieces, axis=0)


def load_own(ref, info, masked):
    piece = ref[info[0]]
    if not masked:
        return piece
    rows = lax.broadcasted_iota(jnp.int32, piece.shape, 0) + info[1] * HD
    return jnp.where(rows < info[2 + info[0]], piece, jnp.zeros_like(piece))


def own_lanes(row, info):
    pieces = [row[:, i * HD : (i + 1) * HD] for i in range(SIDE)]
    return sum(jnp.where(info[0] == i, piece, 0.0) for i, piece in enumerate(pieces))


def causal(info):
    keys = lax.broadcasted_iota(jnp.int32, (L, HD), 0)
    rows = lax.broadcasted_iota(jnp.int32, (L, HD), 1) + info[1] * HD
    return keys <= rows


def local_stats(scores, dprods):
    top = jnp.max(scores, axis=0, keepdims=True)
    weights = jnp.exp2(scores - top)
    total = jnp.sum(weights, axis=0, keepdims=True)
    mixed = jnp.sum(weights * dprods, axis=0, keepdims=True)
    return top, total, mixed


def merge(found):
    top = functools.reduce(jnp.maximum, [item[0] for item in found])
    scales = [jnp.exp2(item[0] - top) for item in found]
    total = sum(item[1] * scale for item, scale in zip(found, scales))
    mixed = sum(item[2] * scale for item, scale in zip(found, scales))
    return top, total, mixed


def stats_kernel(info, q_ref, g_ref, key_ref, value_ref, sk_ref, sv_ref, out_ref):
    head = pl.program_id(0)

    @pl.when(head == 0)
    def _():
        out_ref[...] = jnp.zeros_like(out_ref)

    q = load_rows(q_ref)
    g = load_valid(g_ref, info)
    found = [
        local_stats(dot_nt(key_ref[i], q) * LOG_FACTOR, dot_nt(value_ref[i], g)) for i in range(SIDE)
    ]
    q = load_own(q_ref, info, False)
    g = load_own(g_ref, info, True)
    scores = jnp.where(causal(info), dot_nt(sk_ref[...], q) * LOG_FACTOR, -jnp.inf)
    own = local_stats(scores, dot_nt(sv_ref[...], g))
    mine = lax.broadcasted_iota(jnp.int32, (1, SIDE * HD), 1) // HD == info[0]
    found.append(
        tuple(
            jnp.where(mine, jnp.concatenate([item] * SIDE, axis=1), other)
            for item, other in zip(own, (LOW, 0.0, 0.0))
        )
    )
    found = merge(found)
    for copy in range(SIDE):
        for kind in range(3):
            out_ref[copy, pl.ds(kind * GROUP + head, 1), :] = found[kind]


def score_grads(k, v, q, g, log_sum, delta, allowed=None):
    probs = jnp.exp2(dot_nt(k, q) * LOG_FACTOR - log_sum)
    if allowed is not None:
        probs = jnp.where(allowed, probs, 0.0)
    dscores = (probs * (dot_nt(v, g) - delta)).astype(BF16)
    return probs.astype(BF16), dscores


def grads_kernel(
    info, q_ref, g_ref, key_ref, value_ref, sk_ref, sv_ref, part_ref,
    dq_ref, dk_ref, dv_ref, dsk_ref, dsv_ref, send_ref,
    stat_ref, keyt_ref, skt_ref, dkey_ref, dvalue_ref, dself_key_ref, dself_value_ref,
):
    head = pl.program_id(0)

    @pl.when(head == 0)
    def _():
        parts = [
            tuple(part_ref[i, kind * GROUP : (kind + 1) * GROUP, :] for kind in range(3))
            for i in range(SIDE)
        ]
        top, total, mixed = merge(parts)
        stat_ref[:GROUP, :] = top + jnp.log2(total)
        stat_ref[GROUP : 2 * GROUP, :] = mixed / total
        for i in range(SIDE):
            keyt_ref[i] = key_ref[i].T
        skt_ref[...] = sk_ref[...].T
        dkey_ref[...] = jnp.zeros_like(dkey_ref)
        dvalue_ref[...] = jnp.zeros_like(dvalue_ref)
        dself_key_ref[...] = jnp.zeros_like(dself_key_ref)
        dself_value_ref[...] = jnp.zeros_like(dself_value_ref)

    log_sum = stat_ref[pl.ds(head, 1), :]
    delta = stat_ref[pl.ds(GROUP + head, 1), :]
    q = load_rows(q_ref)
    g = load_valid(g_ref, info)
    dq = jnp.zeros((HD, SIDE * HD), F32)
    for i in range(SIDE):
        probs, dscores = score_grads(key_ref[i], value_ref[i], q, g, log_sum, delta)
        dvalue_ref[i] += dot_nn(probs, g)
        dkey_ref[i] += dot_nn(dscores, q)
        dq = dq + dot_nn(keyt_ref[i], dscores)

    q = load_own(q_ref, info, False)
    g = load_own(g_ref, info, True)
    probs, dscores = score_grads(
        sk_ref[...], sv_ref[...], q, g, own_lanes(log_sum, info), own_lanes(delta, info), causal(info)
    )
    dself_value_ref[...] += dot_nn(probs, g)
    dself_key_ref[...] += dot_nn(dscores, q)
    own = dot_nn(skt_ref[...], dscores)
    for response in range(SIDE):
        piece = dq[:, response * HD : (response + 1) * HD]
        piece = piece + jnp.where(response == info[0], own, 0.0)
        dq_ref[response] = (piece * FACTOR).T.astype(BF16)

    @pl.when(head == GROUP - 1)
    def _():
        mine = info[1]
        slots = pl.ds(pl.multiple_of(mine * HD, HD), HD)
        dk_ref[...] = dkey_ref[mine] * FACTOR
        dv_ref[...] = dvalue_ref[mine]
        dsk_ref[...] = dself_key_ref[slots, :] * FACTOR
        dsv_ref[...] = dself_value_ref[slots, :]
        for i in range(SIDE):
            slots = slice(i * HD, (i + 1) * HD)
            send_ref[i, :L, :HD] = (dkey_ref[i] * FACTOR).astype(BF16)
            send_ref[i, :L, HD:] = dvalue_ref[i].astype(BF16)
            send_ref[i, L:, :HD] = (dself_key_ref[slots, :] * FACTOR).astype(BF16)
            send_ref[i, L:, HD:] = dself_value_ref[slots, :].astype(BF16)
        send_ref[mine] = jnp.zeros(send_ref.shape[1:], BF16)


def finish_kernel(dk_ref, dv_ref, dsk_ref, dsv_ref, back_ref, dk_out, dv_out, dsk_out, dsv_out):
    def total(own_ref, rows, columns):
        return own_ref[...] + sum(back_ref[i, rows, columns].astype(F32) for i in range(SIDE))

    doc, slots = slice(0, L), slice(L, L + HD)
    keys, values = slice(0, HD), slice(HD, 2 * HD)
    dk_out[...] = total(dk_ref, doc, keys)
    dv_out[...] = total(dv_ref, doc, values)
    dsk_out[...] = total(dsk_ref, slots, keys)
    dsv_out[...] = total(dsv_ref, slots, values)


def sum_turn_kernel(parts_ref, out_ref):
    total = parts_ref[0].astype(F32)
    for part in range(1, parts_ref.shape[0]):
        total = total + parts_ref[part].astype(F32)
    out_ref[...] = total.T.astype(BF16)


def project_kernel(info, part_ref, weight_ref, theirs_ref, mine_ref, rows_ref):
    step = pl.program_id(0)

    @pl.when(step == 0)
    def _():
        rows_ref[...] = sum(part_ref[i].astype(F32) for i in range(SIDE)).astype(BF16)

    terms = dot_nt(weight_ref[...], rows_ref[...]).astype(BF16)

    @pl.when(step < SIDE)
    def _():
        theirs_ref[0] = terms

    @pl.when(step >= SIDE)
    def _():
        mine_ref[0] = terms


def params(megabytes=56):
    return pltpu.CompilerParams(vmem_limit_bytes=megabytes * 1024 * 1024)


def body(queries, doc_keys, doc_values, self_keys, self_values, out_grads, lengths, query_weight):
    doc_rows = doc_keys.shape[0]
    info = jnp.concatenate(
        [
            lax.axis_index("z").astype(jnp.int32)[None],
            lax.axis_index("y").astype(jnp.int32)[None],
            lengths.astype(jnp.int32),
            lax.axis_index("core").astype(jnp.int32)[None],
        ]
    )
    q_four = queries.reshape(SIDE, L, WIDTH)
    g_four = out_grads.reshape(SIDE, L, WIDTH)

    weight = lax.all_gather(query_weight, ("z", "y"), axis=0, tiled=True)
    pairs = jnp.concatenate([doc_keys, doc_values], axis=1)
    pairs = jnp.broadcast_to(pairs[None], (SIDE, doc_rows, 2 * HD))
    pairs = lax.all_to_all(pairs, "y", 0, 0, tiled=True)

    rows_spec = pl.BlockSpec((SIDE, HD, HD), lambda h, info: (0, info[1], h))
    keys_spec = pl.BlockSpec((SIDE, doc_rows, HD), lambda h, info: (0, 0, 0))
    values_spec = pl.BlockSpec((SIDE, doc_rows, HD), lambda h, info: (0, 0, 1))
    response_spec = pl.BlockSpec((L, HD), lambda h, info: (info[0], 0))
    stat_spec = pl.BlockSpec((SIDE, STATS, SIDE * HD), lambda h, info: (0, 0, 0))
    in_specs = [rows_spec, rows_spec, keys_spec, values_spec, response_spec, response_spec]
    operands = (info, q_four, g_four, pairs, pairs, self_keys, self_values)
    elements = GROUP * SIDE * HD * doc_rows * SIDE

    stats = pl.pallas_call(
        stats_kernel,
        grid_spec=pltpu.PrefetchScalarGridSpec(
            num_scalar_prefetch=1, grid=(GROUP,), in_specs=in_specs, out_specs=stat_spec
        ),
        out_shape=jax.ShapeDtypeStruct((SIDE, STATS, SIDE * HD), F32),
        compiler_params=params(),
        cost_estimate=pl.CostEstimate(
            flops=4 * elements * HD, bytes_accessed=2**22, transcendentals=elements
        ),
        name="local_stats",
    )(*operands)
    parts = lax.all_to_all(stats, "z", 0, 0, tiled=True)

    fixed = lambda *shape: pl.BlockSpec(shape, lambda h, info: (0,) * len(shape))
    dq, dk, dv, dsk, dsv, sends = pl.pallas_call(
        grads_kernel,
        grid_spec=pltpu.PrefetchScalarGridSpec(
            num_scalar_prefetch=1,
            grid=(GROUP,),
            in_specs=in_specs + [stat_spec],
            out_specs=[
                pl.BlockSpec((SIDE, HD, HD), lambda h, info: (0, 0, h)),
                fixed(doc_rows, HD), fixed(doc_rows, HD), fixed(HD, HD), fixed(HD, HD),
                fixed(SIDE, doc_rows + HD, 2 * HD),
            ],
            scratch_shapes=[
                pltpu.VMEM((STATS, SIDE * HD), F32),
                pltpu.VMEM((SIDE, HD, doc_rows), BF16),
                pltpu.VMEM((HD, L), BF16),
                pltpu.VMEM((SIDE, doc_rows, HD), F32),
                pltpu.VMEM((SIDE, doc_rows, HD), F32),
                pltpu.VMEM((L, HD), F32),
                pltpu.VMEM((L, HD), F32),
            ],
        ),
        out_shape=[jax.ShapeDtypeStruct((SIDE, HD, WIDTH), BF16)]
        + [jax.ShapeDtypeStruct((doc_rows, HD), F32)] * 2
        + [jax.ShapeDtypeStruct((HD, HD), F32)] * 2
        + [jax.ShapeDtypeStruct((SIDE, doc_rows + HD, 2 * HD), BF16)],
        compiler_params=params(),
        cost_estimate=pl.CostEstimate(
            flops=10 * elements * HD, bytes_accessed=2**23, transcendentals=elements
        ),
        name="local_grads",
    )(*operands, parts)

    dq_parts = lax.all_to_all(dq, "z", 0, 0, tiled=True)
    back = lax.all_to_all(sends, "y", 0, 0, tiled=True)
    columns = 2 * query_weight.shape[0]

    def weight_block(i, info):
        core = info[2 + SIDE]
        return 2 * lax.rem(i, SIDE) + jnp.where(i < SIDE, 1 - core, core), 0

    theirs, mine = pl.pallas_call(
        project_kernel,
        grid_spec=pltpu.PrefetchScalarGridSpec(
            num_scalar_prefetch=1,
            grid=(2 * SIDE,),
            in_specs=[fixed(SIDE, HD, WIDTH), pl.BlockSpec((columns, WIDTH), weight_block)],
            out_specs=[
                pl.BlockSpec((1, columns, HD), lambda i, info: (jnp.minimum(i, SIDE - 1), 0, 0)),
                pl.BlockSpec((1, columns, HD), lambda i, info: (jnp.maximum(i - SIDE, 0), 0, 0)),
            ],
            scratch_shapes=[pltpu.VMEM((HD, WIDTH), BF16)],
        ),
        out_shape=[jax.ShapeDtypeStruct((SIDE, columns, HD), BF16)] * 2,
        compiler_params=params(),
        name="project",
    )(info, dq_parts, weight)
    theirs = lax.ppermute(theirs, "core", [(0, 1), (1, 0)])
    terms = (mine.astype(F32) + theirs.astype(F32)).astype(BF16)
    terms = lax.all_to_all(terms, "x", 0, 0, tiled=True)
    input_grads = pl.pallas_call(
        sum_turn_kernel,
        out_shape=jax.ShapeDtypeStruct((HD, columns), BF16),
        name="sum_groups",
    )(terms)
    dk, dv, dsk, dsv = pl.pallas_call(
        finish_kernel,
        out_shape=[jax.ShapeDtypeStruct((doc_rows, HD), F32)] * 2
        + [jax.ShapeDtypeStruct((HD, HD), F32)] * 2,
        name="sum_key_values",
    )(dk, dv, dsk, dsv, back)
    return input_grads, dk, dv, dsk, dsv


def solution(mesh):
    grid = Mesh(mesh.devices.reshape(SIDE, SIDE, SIDE, 2), ("z", "y", "x", "core"))
    seq, head = ("z", "y"), ("x", "core")
    in_specs = (
        P(None, head),
        P(seq, head),
        P(seq, head),
        P(None, head),
        P(None, head),
        P(None, head),
        P(),
        P(seq, head),
    )
    return jax.shard_map(
        body, mesh=grid, in_specs=in_specs, out_specs=(P(seq, head),) * 5, check_vma=False
    )
```

```python
import functools
import math

import jax
import jax.numpy as jnp
from jax import lax
from jax.experimental import pallas as pl
from jax.experimental.pallas import tpu as pltpu
from jax.sharding import Mesh, PartitionSpec as P

HQ = 40
KVH = 8
HD = 128
L = 512
GROUP = HQ // KVH
WIDTH = GROUP * HD
FACTOR = HD ** (-0.5)
LOG_FACTOR = FACTOR * math.log2(math.e)
STATS = 16
SIDE = 4
LOW = -1e30
BF16 = jnp.bfloat16
F32 = jnp.float32


def dot_nt(a, b):
    return lax.dot_general(a, b, (((1,), (1,)), ((), ())), preferred_element_type=F32)


def dot_nn(a, b):
    return lax.dot_general(a, b, (((1,), (0,)), ((), ())), preferred_element_type=F32)


def head_lanes(head):
    return pl.ds(pl.multiple_of(head * HD, HD), HD)


def load_head(ref, head):
    return ref[:, :, head_lanes(head)].reshape(SIDE * HD, HD)


def load_own(ref, info):
    own = ref[info[0]]
    return jnp.concatenate([own[:, h * HD : (h + 1) * HD] for h in range(GROUP)], axis=0)


def own_lanes(row, info):
    pieces = [row[:, i * HD : (i + 1) * HD] for i in range(SIDE)]
    return sum(jnp.where(info[0] == i, piece, 0.0) for i, piece in enumerate(pieces))


def response_rows(info):
    return pl.ds(pl.multiple_of(info[0] * L, L), L)


def causal(info):
    keys = lax.broadcasted_iota(jnp.int32, (L, HD), 0)
    rows = lax.broadcasted_iota(jnp.int32, (L, HD), 1) + info[1] * HD
    return jnp.concatenate([keys <= rows] * GROUP, axis=1)


def local_stats(scores, dprods):
    top = jnp.max(scores, axis=0, keepdims=True)
    weights = jnp.exp2(scores - top)
    total = jnp.sum(weights, axis=0, keepdims=True)
    mixed = jnp.sum(weights * dprods, axis=0, keepdims=True)
    return top, total, mixed


def merge(found):
    top = functools.reduce(jnp.maximum, [item[0] for item in found])
    scales = [jnp.exp2(item[0] - top) for item in found]
    total = sum(item[1] * scale for item, scale in zip(found, scales))
    mixed = sum(item[2] * scale for item, scale in zip(found, scales))
    return top, total, mixed


def block_stats(q, g, keys, values):
    return local_stats(dot_nt(keys, q) * LOG_FACTOR, dot_nt(values, g))


def put_stats(ref, head, found):
    for kind in range(3):
        ref[pl.ds(kind * GROUP + head, 1), :] = found[kind]


def get_stats(ref, head):
    return tuple(ref[pl.ds(kind * GROUP + head, 1), :] for kind in range(3))


def own_stats_kernel(info, q_ref, g_ref, key_ref, value_ref, sk_ref, sv_ref, out_ref):
    out_ref[...] = jnp.zeros_like(out_ref)
    scores = dot_nt(sk_ref[response_rows(info), :], load_own(q_ref, info)) * LOG_FACTOR
    scores = jnp.where(causal(info), scores, -jnp.inf)
    own = local_stats(scores, dot_nt(sv_ref[response_rows(info), :], load_own(g_ref, info)))
    mine = lax.broadcasted_iota(jnp.int32, (1, SIDE * HD), 1) // HD == info[0]
    for head in range(GROUP):
        wide = [jnp.concatenate([item[:, head * HD : (head + 1) * HD]] * SIDE, axis=1) for item in own]
        put_stats(out_ref, head, [jnp.where(mine, a, b) for a, b in zip(wide, (LOW, 0.0, 0.0))])

    @pl.loop(0, GROUP)
    def _(head):
        found = block_stats(load_head(q_ref, head), load_head(g_ref, head), key_ref[...], value_ref[...])
        put_stats(out_ref, head, merge([found, get_stats(out_ref, head)]))


def rest_stats_kernel(info, q_ref, g_ref, pair_ref, former_ref, out_ref):
    out_ref[...] = jnp.zeros_like(out_ref)

    @pl.loop(0, GROUP)
    def _(head):
        q, g = load_head(q_ref, head), load_head(g_ref, head)
        found = [get_stats(former_ref, head)]
        for step in range(1, SIDE):
            i = lax.rem(info[1] + step, SIDE)
            found.append(block_stats(q, g, pair_ref[i, :, :HD], pair_ref[i, :, HD:]))
        found = merge(found)
        for copy in range(SIDE):
            put_stats(out_ref.at[copy], head, found)


def score_grads(k, v, q, g, log_sum, delta, allowed=None):
    probs = jnp.exp2(dot_nt(k, q) * LOG_FACTOR - log_sum)
    if allowed is not None:
        probs = jnp.where(allowed, probs, 0.0)
    dscores = (probs * (dot_nt(v, g) - delta)).astype(BF16)
    return probs.astype(BF16), dscores


def grads_kernel(
    info, q_ref, g_ref, pair_ref, sk_ref, sv_ref, part_ref,
    dq_ref, dk_ref, dv_ref, dsk_ref, dsv_ref, send_ref,
    stat_ref, keyt_ref, dkey_ref, dvalue_ref, dself_key_ref, dself_value_ref, dself_query_ref,
):
    parts = [
        tuple(part_ref[i, kind * GROUP : (kind + 1) * GROUP, :] for kind in range(3)) for i in range(SIDE)
    ]
    top, total, mixed = merge(parts)
    stat_ref[:GROUP, :] = top + jnp.log2(total)
    stat_ref[GROUP : 2 * GROUP, :] = mixed / total
    for i in range(SIDE):
        keyt_ref[i] = pair_ref[i, :, :HD].T
    dkey_ref[...] = jnp.zeros_like(dkey_ref)
    dvalue_ref[...] = jnp.zeros_like(dvalue_ref)

    q, g = load_own(q_ref, info), load_own(g_ref, info)
    keys = sk_ref[response_rows(info), :]
    log_sum, delta = (
        jnp.concatenate([own_lanes(stat_ref[first + h : first + h + 1, :], info) for h in range(GROUP)], axis=1)
        for first in (0, GROUP)
    )
    probs, dscores = score_grads(
        keys, sv_ref[response_rows(info), :], q, g, log_sum, delta, causal(info)
    )
    dself_value_ref[...] = dot_nn(probs, g)
    dself_key_ref[...] = dot_nn(dscores, q)
    dself_query_ref[...] = dot_nn(keys.T, dscores)

    @pl.loop(0, GROUP)
    def _(head):
        log_sum = stat_ref[pl.ds(head, 1), :]
        delta = stat_ref[pl.ds(GROUP + head, 1), :]
        q, g = load_head(q_ref, head), load_head(g_ref, head)
        dq = jnp.zeros((HD, SIDE * HD), F32)
        for i in range(SIDE):
            probs, dscores = score_grads(pair_ref[i, :, :HD], pair_ref[i, :, HD:], q, g, log_sum, delta)
            dvalue_ref[i] += dot_nn(probs, g)
            dkey_ref[i] += dot_nn(dscores, q)
            dq = dq + dot_nn(keyt_ref[i], dscores)
        own = dself_query_ref[:, head_lanes(head)]
        for response in range(SIDE):
            piece = dq[:, response * HD : (response + 1) * HD]
            piece = piece + jnp.where(response == info[0], own, 0.0)
            dq_ref[response, :, head_lanes(head)] = (piece * FACTOR).T.astype(BF16)

    mine = info[1]
    slots = pl.ds(pl.multiple_of(mine * HD, HD), HD)
    dk_ref[...] = dkey_ref[mine] * FACTOR
    dv_ref[...] = dvalue_ref[mine]
    dsk_ref[...] = dself_key_ref[slots, :] * FACTOR
    dsv_ref[...] = dself_value_ref[slots, :]
    for i in range(SIDE):
        slots = slice(i * HD, (i + 1) * HD)
        send_ref[i, :L, :HD] = (dkey_ref[i] * FACTOR).astype(BF16)
        send_ref[i, :L, HD:] = dvalue_ref[i].astype(BF16)
        send_ref[i, L:, :HD] = (dself_key_ref[slots, :] * FACTOR).astype(BF16)
        send_ref[i, L:, HD:] = dself_value_ref[slots, :].astype(BF16)
    send_ref[mine] = jnp.zeros(send_ref.shape[1:], BF16)


def finish_kernel(dk_ref, dv_ref, dsk_ref, dsv_ref, back_ref, dk_out, dv_out, dsk_out, dsv_out):
    def total(own_ref, rows, columns):
        return own_ref[...] + sum(back_ref[i, rows, columns].astype(F32) for i in range(SIDE))

    doc, slots = slice(0, L), slice(L, L + HD)
    keys, values = slice(0, HD), slice(HD, 2 * HD)
    dk_out[...] = total(dk_ref, doc, keys)
    dv_out[...] = total(dv_ref, doc, values)
    dsk_out[...] = total(dsk_ref, slots, keys)
    dsv_out[...] = total(dsv_ref, slots, values)


def sum_turn_kernel(parts_ref, out_ref):
    total = parts_ref[0].astype(F32)
    for part in range(1, parts_ref.shape[0]):
        total = total + parts_ref[part].astype(F32)
    out_ref[...] = total.T.astype(BF16)


def project_blocks(weight_hbm, buffer, sems, core, rows, put):
    depth = buffer.shape[1]

    def fetch(i):
        at = pl.ds(pl.multiple_of((2 * i + core) * depth, depth), depth)
        return pltpu.make_async_copy(weight_hbm.at[at], buffer.at[i], sems.at[i])

    for i in range(SIDE):
        fetch(i).start()
    rows = rows()
    for i in range(SIDE):
        fetch(i).wait()
        put(i, dot_nt(buffer[i], rows))


def project_theirs_kernel(info, part_ref, weight_hbm, out_ref, rows_ref, buffer, sems):
    def rows():
        rows_ref[...] = sum(part_ref[i].astype(F32) for i in range(SIDE)).astype(BF16)
        return rows_ref[...]

    def put(i, terms):
        out_ref[i] = terms.astype(BF16)

    project_blocks(weight_hbm, buffer, sems, 1 - info[2], rows, put)


def project_mine_kernel(info, rows_ref, theirs_ref, weight_hbm, out_ref, buffer, sems):
    def put(i, terms):
        out_ref[i] = (terms + theirs_ref[i].astype(F32)).astype(BF16)

    project_blocks(weight_hbm, buffer, sems, info[2], lambda: rows_ref[...], put)


def params(megabytes):
    return pltpu.CompilerParams(vmem_limit_bytes=megabytes * 1024 * 1024)


def body(queries, doc_keys, doc_values, self_keys, self_values, out_grads, lengths, query_weight):
    doc_rows = doc_keys.shape[0]
    place_y = lax.axis_index("y").astype(jnp.int32)
    info = jnp.stack([lax.axis_index("z").astype(jnp.int32), place_y, lax.axis_index("core").astype(jnp.int32)])
    weight = lax.all_gather(query_weight, ("z", "y"), axis=0, tiled=True)
    pairs = jnp.concatenate([doc_keys, doc_values], axis=1)
    pairs = jnp.broadcast_to(pairs[None], (SIDE, doc_rows, 2 * HD))
    pairs = lax.all_to_all(pairs, "y", 0, 0, tiled=True)

    def own_rows(array):
        return lax.dynamic_slice_in_dim(array.reshape(SIDE, L, WIDTH), place_y * HD, HD, 1)

    valid = (jnp.arange(HD, dtype=jnp.int32) + place_y * HD)[None, :] < lengths[:, None]
    q_own = own_rows(queries)
    g_own = own_rows(out_grads) * valid[..., None].astype(out_grads.dtype)

    smem = pl.BlockSpec(memory_space=pltpu.SMEM)
    vmem = pl.BlockSpec(memory_space=pltpu.VMEM)
    anywhere = pl.BlockSpec(memory_space=pl.ANY)
    elements = GROUP * SIDE * HD * doc_rows

    def cost(products, blocks):
        return pl.CostEstimate(
            flops=2 * products * blocks * elements * HD,
            bytes_accessed=2**21,
            transcendentals=blocks * elements,
        )

    stats = pl.pallas_call(
        own_stats_kernel,
        in_specs=[smem] + [vmem] * 6,
        out_specs=vmem,
        out_shape=jax.ShapeDtypeStruct((STATS, SIDE * HD), F32),
        compiler_params=params(20),
        cost_estimate=cost(2, 1),
        name="own_stats",
    )(info, q_own, g_own, doc_keys, doc_values, self_keys, self_values)
    stats = pl.pallas_call(
        rest_stats_kernel,
        in_specs=[smem] + [vmem] * 4,
        out_specs=vmem,
        out_shape=jax.ShapeDtypeStruct((SIDE, STATS, SIDE * HD), F32),
        compiler_params=params(20),
        cost_estimate=cost(2, 3),
        name="rest_stats",
    )(info, q_own, g_own, pairs, stats)
    parts = lax.all_to_all(stats, "z", 0, 0, tiled=True)

    dq, dk, dv, dsk, dsv, sends = pl.pallas_call(
        grads_kernel,
        in_specs=[smem] + [vmem] * 6,
        out_specs=[vmem] * 6,
        scratch_shapes=[
            pltpu.VMEM((STATS, SIDE * HD), F32),
            pltpu.VMEM((SIDE, HD, doc_rows), BF16),
            pltpu.VMEM((SIDE, doc_rows, HD), F32),
            pltpu.VMEM((SIDE, doc_rows, HD), F32),
            pltpu.VMEM((L, HD), F32),
            pltpu.VMEM((L, HD), F32),
            pltpu.VMEM((HD, WIDTH), F32),
        ],
        out_shape=[jax.ShapeDtypeStruct((SIDE, HD, WIDTH), BF16)]
        + [jax.ShapeDtypeStruct((doc_rows, HD), F32)] * 2
        + [jax.ShapeDtypeStruct((HD, HD), F32)] * 2
        + [jax.ShapeDtypeStruct((SIDE, doc_rows + HD, 2 * HD), BF16)],
        compiler_params=params(28),
        cost_estimate=cost(5, SIDE),
        name="local_grads",
    )(info, q_own, g_own, pairs, self_keys, self_values, parts)

    dq_parts = lax.all_to_all(dq, "z", 0, 0, tiled=True)
    back = lax.all_to_all(sends, "y", 0, 0, tiled=True)
    columns = 2 * query_weight.shape[0]
    terms_shape = jax.ShapeDtypeStruct((SIDE, columns, HD), BF16)
    scratch = [pltpu.VMEM((SIDE, columns, WIDTH), BF16), pltpu.SemaphoreType.DMA((SIDE,))]
    project_cost = pl.CostEstimate(
        flops=SIDE * columns * WIDTH * HD * 2, bytes_accessed=2**22, transcendentals=0
    )
    theirs, rows = pl.pallas_call(
        project_theirs_kernel,
        in_specs=[smem, vmem, anywhere],
        out_specs=[vmem] * 2,
        out_shape=[terms_shape, jax.ShapeDtypeStruct((HD, WIDTH), BF16)],
        scratch_shapes=scratch,
        compiler_params=params(24),
        cost_estimate=project_cost,
        name="project_theirs",
    )(info, dq_parts, weight)
    theirs = lax.ppermute(theirs, "core", [(0, 1), (1, 0)])
    terms = pl.pallas_call(
        project_mine_kernel,
        in_specs=[smem, vmem, vmem, anywhere],
        out_specs=vmem,
        out_shape=terms_shape,
        scratch_shapes=scratch,
        compiler_params=params(24),
        cost_estimate=project_cost,
        name="project_mine",
    )(info, rows, theirs, weight)
    terms = lax.all_to_all(terms, "x", 0, 0, tiled=True)
    input_grads = pl.pallas_call(
        sum_turn_kernel,
        out_shape=jax.ShapeDtypeStruct((HD, columns), BF16),
        name="sum_groups",
    )(terms)
    dk, dv, dsk, dsv = pl.pallas_call(
        finish_kernel,
        out_shape=[jax.ShapeDtypeStruct((doc_rows, HD), F32)] * 2
        + [jax.ShapeDtypeStruct((HD, HD), F32)] * 2,
        name="sum_key_values",
    )(dk, dv, dsk, dsv, back)
    return input_grads, dk, dv, dsk, dsv


def solution(mesh):
    grid = Mesh(mesh.devices.reshape(SIDE, SIDE, SIDE, 2), ("z", "y", "x", "core"))
    seq, head = ("z", "y"), ("x", "core")
    in_specs = (
        P(None, head),
        P(seq, head),
        P(seq, head),
        P(None, head),
        P(None, head),
        P(None, head),
        P(),
        P(seq, head),
    )
    return jax.shard_map(
        body, mesh=grid, in_specs=in_specs, out_specs=(P(seq, head),) * 5, check_vma=False
    )
```

```python
import functools
import math

import jax
import jax.numpy as jnp
from jax import lax
from jax.experimental import pallas as pl
from jax.experimental.pallas import tpu as pltpu
from jax.sharding import Mesh, PartitionSpec as P

HQ = 40
KVH = 8
HD = 128
L = 512
GROUP = HQ // KVH
WIDTH = GROUP * HD
FACTOR = HD ** (-0.5)
LOG_FACTOR = FACTOR * math.log2(math.e)
STATS = 16
SIDE = 4
LOW = -1e30
PLACES = (1, 3, 2)
Z = ("z_high", "z_low")
BF16 = jnp.bfloat16
F32 = jnp.float32


def dot_nt(a, b):
    return lax.dot_general(a, b, (((1,), (1,)), ((), ())), preferred_element_type=F32)


def dot_nn(a, b):
    return lax.dot_general(a, b, (((1,), (0,)), ((), ())), preferred_element_type=F32)


def head_lanes(head):
    return pl.ds(pl.multiple_of(head * HD, HD), HD)


def load_head(ref, head):
    return ref[:, :, head_lanes(head)].reshape(SIDE * HD, HD)


def load_own(ref, info):
    own = ref[info[0]]
    return jnp.concatenate([own[:, h * HD : (h + 1) * HD] for h in range(GROUP)], axis=0)


def own_lanes(row, info):
    pieces = [row[:, i * HD : (i + 1) * HD] for i in range(SIDE)]
    return sum(jnp.where(info[0] == i, piece, 0.0) for i, piece in enumerate(pieces))


def response_rows(info):
    return pl.ds(pl.multiple_of(info[0] * L, L), L)


def causal(info):
    keys = lax.broadcasted_iota(jnp.int32, (L, HD), 0)
    rows = lax.broadcasted_iota(jnp.int32, (L, HD), 1) + info[1] * HD
    return jnp.concatenate([keys <= rows] * GROUP, axis=1)


def local_stats(scores, dprods):
    top = jnp.max(scores, axis=0, keepdims=True)
    weights = jnp.exp2(scores - top)
    total = jnp.sum(weights, axis=0, keepdims=True)
    mixed = jnp.sum(weights * dprods, axis=0, keepdims=True)
    return top, total, mixed


def merge(found):
    top = functools.reduce(jnp.maximum, [item[0] for item in found])
    scales = [jnp.exp2(item[0] - top) for item in found]
    total = sum(item[1] * scale for item, scale in zip(found, scales))
    mixed = sum(item[2] * scale for item, scale in zip(found, scales))
    return top, total, mixed


def block_stats(q, g, keys, values):
    return local_stats(dot_nt(keys, q) * LOG_FACTOR, dot_nt(values, g))


def put_stats(ref, head, found):
    for kind in range(3):
        ref[pl.ds(kind * GROUP + head, 1), :] = found[kind]


def get_stats(ref, head):
    return tuple(ref[pl.ds(kind * GROUP + head, 1), :] for kind in range(3))


def own_stats_kernel(info, q_ref, g_ref, pair_ref, sk_ref, sv_ref, out_ref):
    out_ref[...] = jnp.zeros_like(out_ref)
    scores = dot_nt(sk_ref[response_rows(info), :], load_own(q_ref, info)) * LOG_FACTOR
    scores = jnp.where(causal(info), scores, -jnp.inf)
    own = local_stats(scores, dot_nt(sv_ref[response_rows(info), :], load_own(g_ref, info)))
    mine = lax.broadcasted_iota(jnp.int32, (1, SIDE * HD), 1) // HD == info[0]
    for head in range(GROUP):
        wide = [jnp.concatenate([item[:, head * HD : (head + 1) * HD]] * SIDE, axis=1) for item in own]
        put_stats(out_ref, head, [jnp.where(mine, a, b) for a, b in zip(wide, (LOW, 0.0, 0.0))])

    @pl.loop(0, GROUP)
    def _(head):
        found = block_stats(load_head(q_ref, head), load_head(g_ref, head), pair_ref[0], pair_ref[1])
        put_stats(out_ref, head, merge([found, get_stats(out_ref, head)]))


def rest_stats_kernel(info, q_ref, g_ref, p1_ref, p2_ref, p3_ref, former_ref, out_ref):
    out_ref[...] = jnp.zeros_like(out_ref)

    @pl.loop(0, GROUP)
    def _(head):
        q, g = load_head(q_ref, head), load_head(g_ref, head)
        found = [get_stats(former_ref, head)]
        for ref in (p1_ref, p2_ref, p3_ref):
            found.append(block_stats(q, g, ref[0], ref[1]))
        found = merge(found)
        for copy in range(SIDE):
            put_stats(out_ref.at[copy], head, found)


def score_grads(k, v, q, g, log_sum, delta, allowed=None):
    probs = jnp.exp2(dot_nt(k, q) * LOG_FACTOR - log_sum)
    if allowed is not None:
        probs = jnp.where(allowed, probs, 0.0)
    dscores = (probs * (dot_nt(v, g) - delta)).astype(BF16)
    return probs.astype(BF16), dscores


def grads_kernel(
    info, q_ref, g_ref, p0_ref, p1_ref, p2_ref, p3_ref, sk_ref, sv_ref, part_ref,
    dq0_ref, dq1_ref, dq2_ref, dq3_ref, own_ref, send1_ref, send2_ref, send3_ref,
    stat_ref, keyt_ref, dkey_ref, dvalue_ref, dself_key_ref, dself_value_ref, dself_query_ref, piece_ref,
):
    pair_refs = (p0_ref, p1_ref, p2_ref, p3_ref)
    parts = [
        tuple(part_ref[i, kind * GROUP : (kind + 1) * GROUP, :] for kind in range(3)) for i in range(SIDE)
    ]
    top, total, mixed = merge(parts)
    stat_ref[:GROUP, :] = top + jnp.log2(total)
    stat_ref[GROUP : 2 * GROUP, :] = mixed / total
    for i in range(SIDE):
        keyt_ref[i] = pair_refs[i][0].T
    dkey_ref[...] = jnp.zeros_like(dkey_ref)
    dvalue_ref[...] = jnp.zeros_like(dvalue_ref)

    q, g = load_own(q_ref, info), load_own(g_ref, info)
    keys = sk_ref[response_rows(info), :]
    log_sum, delta = (
        jnp.concatenate([own_lanes(stat_ref[first + h : first + h + 1, :], info) for h in range(GROUP)], axis=1)
        for first in (0, GROUP)
    )
    probs, dscores = score_grads(
        keys, sv_ref[response_rows(info), :], q, g, log_sum, delta, causal(info)
    )
    dself_value_ref[...] = dot_nn(probs, g)
    dself_key_ref[...] = dot_nn(dscores, q)
    dself_query_ref[...] = dot_nn(keys.T, dscores)

    @pl.loop(0, GROUP)
    def _(head):
        log_sum = stat_ref[pl.ds(head, 1), :]
        delta = stat_ref[pl.ds(GROUP + head, 1), :]
        q, g = load_head(q_ref, head), load_head(g_ref, head)
        dq = jnp.zeros((HD, SIDE * HD), F32)
        for i in range(SIDE):
            probs, dscores = score_grads(pair_refs[i][0], pair_refs[i][1], q, g, log_sum, delta)
            dvalue_ref[i] += dot_nn(probs, g)
            dkey_ref[i] += dot_nn(dscores, q)
            dq = dq + dot_nn(keyt_ref[i], dscores)
        own = dself_query_ref[:, head_lanes(head)]
        for response in range(SIDE):
            piece = dq[:, response * HD : (response + 1) * HD]
            piece = piece + jnp.where(response == info[0], own, 0.0)
            piece_ref[response] = (piece * FACTOR).T.astype(BF16)
        for step, out_ref in zip((0,) + PLACES, (dq0_ref, dq1_ref, dq2_ref, dq3_ref)):
            response = lax.rem(info[0] + step, SIDE)
            out_ref[0, :, head_lanes(head)] = piece_ref[response]
            out_ref[1, :, head_lanes(head)] = piece_ref[response ^ 1]

    for i, step, ref in zip(range(SIDE), (0,) + PLACES, (own_ref, send1_ref, send2_ref, send3_ref)):
        source = lax.rem(info[1] + SIDE - step, SIDE)
        slots = pl.ds(pl.multiple_of(source * HD, HD), HD)
        ref[:L, :HD] = (dkey_ref[i] * FACTOR).astype(ref.dtype)
        ref[:L, HD:] = dvalue_ref[i].astype(ref.dtype)
        ref[L:, :HD] = (dself_key_ref[slots, :] * FACTOR).astype(ref.dtype)
        ref[L:, HD:] = dself_value_ref[slots, :].astype(ref.dtype)


def finish_kernel(own_ref, b1_ref, b2_ref, b3_ref, dk_ref, dv_ref, dsk_ref, dsv_ref):
    total = own_ref[...] + sum(ref[...].astype(F32) for ref in (b1_ref, b2_ref, b3_ref))
    dk_ref[...] = total[:L, :HD]
    dv_ref[...] = total[:L, HD:]
    dsk_ref[...] = total[L:, :HD]
    dsv_ref[...] = total[L:, HD:]


def sum_turn_kernel(parts_ref, out_ref):
    total = parts_ref[0].astype(F32)
    for part in range(1, parts_ref.shape[0]):
        total = total + parts_ref[part].astype(F32)
    out_ref[...] = total.T.astype(BF16)


def project_blocks(info, weight_refs, core, rows, put):
    depth = weight_refs[0].shape[1]
    for step, weight_ref in zip((0,) + PLACES, weight_refs):
        source = lax.rem(info[1] + SIDE - step, SIDE)
        at = pl.ds(pl.multiple_of(lax.rem(source, 2) * depth, depth), depth)

        @pl.when(lax.div(source, 2) == core)
        def _():
            for block in range(2):
                terms = dot_nt(weight_ref[block], rows)
                for part in range(2):
                    put(part, block, at, terms[:, part * HD : (part + 1) * HD])


def project_theirs_kernel(
    info, d0_ref, d1_ref, d2_ref, d3_ref, w0_ref, w1_ref, w2_ref, w3_ref, out_ref, rows_ref
):
    for part in range(2):
        total = sum(ref[part].astype(F32) for ref in (d0_ref, d1_ref, d2_ref, d3_ref))
        rows_ref[part * HD : (part + 1) * HD, :] = total.astype(BF16)

    def put(part, block, at, terms):
        out_ref[part, block, at, :] = terms.astype(BF16)

    project_blocks(info, (w0_ref, w1_ref, w2_ref, w3_ref), 1 - info[2], rows_ref[...], put)


def project_mine_kernel(
    info, rows_ref, theirs_ref, w0_ref, w1_ref, w2_ref, w3_ref, out_ref
):
    columns = (info[0], SIDE - 1 - info[0])

    def put(part, block, at, terms):
        terms = terms + theirs_ref[part, block, at, :].astype(F32)
        out_ref[columns[block] ^ part, at, :] = terms.astype(BF16)

    project_blocks(info, (w0_ref, w1_ref, w2_ref, w3_ref), info[2], rows_ref[...], put)


def ring(step):
    return [(i, (i + step) % SIDE) for i in range(SIDE)]


def spread(array, axis):
    return [lax.ppermute(array, axis, ring(step)) for step in PLACES]


def body(queries, doc_keys, doc_values, self_keys, self_values, out_grads, lengths, query_weight):
    doc_rows = doc_keys.shape[0]
    place_y = lax.axis_index("y").astype(jnp.int32)
    info = jnp.stack([lax.axis_index(Z).astype(jnp.int32), place_y, lax.axis_index("core").astype(jnp.int32)])
    pair = jnp.stack([doc_keys, doc_values])
    pairs = [pair] + spread(pair, "y")
    other = lax.ppermute(query_weight, Z, [(i, SIDE - 1 - i) for i in range(SIDE)])

    def own_rows(array):
        return lax.dynamic_slice_in_dim(array.reshape(SIDE, L, WIDTH), place_y * HD, HD, 1)

    valid = (jnp.arange(HD, dtype=jnp.int32) + place_y * HD)[None, :] < lengths[:, None]
    q_own = own_rows(queries)
    g_own = own_rows(out_grads) * valid[..., None].astype(out_grads.dtype)

    smem = pl.BlockSpec(memory_space=pltpu.SMEM)
    vmem = pl.BlockSpec(memory_space=pltpu.VMEM)

    def call(kernel, shapes, operands, name, megabytes=8, scratch=()):
        return pl.pallas_call(
            kernel,
            in_specs=[smem if a is info else vmem for a in operands],
            out_specs=jax.tree.map(lambda _: vmem, shapes),
            out_shape=shapes,
            scratch_shapes=scratch,
            compiler_params=pltpu.CompilerParams(vmem_limit_bytes=megabytes * 1024 * 1024),
            name=name,
        )(*operands)

    shape = jax.ShapeDtypeStruct
    stats = call(
        own_stats_kernel,
        shape((STATS, SIDE * HD), F32),
        (info, q_own, g_own, pair, self_keys, self_values),
        "own_stats",
    )
    weight = jnp.stack([query_weight, other])
    weight, stats, *pairs = lax.optimization_barrier((weight, stats, *pairs))
    weights = [weight] + spread(weight, "y")
    stats = call(
        rest_stats_kernel,
        shape((SIDE, STATS, SIDE * HD), F32),
        (info, q_own, g_own, *pairs[1:], stats),
        "rest_stats",
    )
    parts = lax.all_to_all(stats, Z, 0, 0, tiled=True)

    grad_shape = shape((2, HD, WIDTH), BF16)
    back_shape = shape((doc_rows + HD, 2 * HD), BF16)
    found = call(
        grads_kernel,
        [grad_shape] * SIDE + [shape(back_shape.shape, F32)] + [back_shape] * 3,
        (info, q_own, g_own, *pairs, self_keys, self_values, parts),
        "local_grads",
        megabytes=14,
        scratch=[
            pltpu.VMEM((STATS, SIDE * HD), F32),
            pltpu.VMEM((SIDE, HD, doc_rows), BF16),
            pltpu.VMEM((SIDE, doc_rows, HD), F32),
            pltpu.VMEM((SIDE, doc_rows, HD), F32),
            pltpu.VMEM((L, HD), F32),
            pltpu.VMEM((L, HD), F32),
            pltpu.VMEM((HD, WIDTH), F32),
            pltpu.VMEM((SIDE, HD, HD), BF16),
        ],
    )
    found, weights = lax.optimization_barrier((found, weights))
    dq, dq_sends, own, sends = found[0], found[1:SIDE], found[SIDE], found[SIDE + 1 :]
    dq_parts = [lax.ppermute(a, Z, ring(step)) for step, a in zip(PLACES, dq_sends)]
    backs = [lax.ppermute(a, "y", ring(SIDE - step)) for step, a in zip(PLACES, sends)]
    dq_parts, backs = lax.optimization_barrier((dq_parts, backs))
    columns = 2 * query_weight.shape[0]
    theirs, rows = call(
        project_theirs_kernel,
        [shape((2, 2, columns, HD), BF16), shape((2 * HD, WIDTH), BF16)],
        (info, dq, *dq_parts, *weights),
        "project_theirs",
    )
    theirs = lax.ppermute(theirs, "core", [(0, 1), (1, 0)])
    terms = call(
        project_mine_kernel,
        shape((SIDE, columns, HD), BF16),
        (info, rows, theirs, *weights),
        "project_mine",
    )
    terms = lax.all_to_all(terms, "x", 0, 0, tiled=True)
    input_grads = call(sum_turn_kernel, shape((HD, columns), BF16), (terms,), "sum_groups")
    moves = []
    for z in range(SIDE):
        for x in range(SIDE):
            stays = x in (z, SIDE - 1 - z)
            moves.append((z * SIDE + x, z * SIDE + x if stays else (z ^ 1) * SIDE + (x ^ 1)))
    input_grads = lax.ppermute(input_grads, Z + ("x",), moves)
    grads = call(
        finish_kernel,
        [shape((doc_rows, HD), F32)] * 2 + [shape((HD, HD), F32)] * 2,
        (own, *backs),
        "sum_key_values",
    )
    return (input_grads, *grads)


def solution(mesh):
    names = ("z_high", "z_low", "y", "x", "core")
    grid = Mesh(mesh.devices.reshape(2, 2, SIDE, SIDE, 2), names)
    seq, head = names[:3], names[3:]
    in_specs = (
        P(None, head),
        P(seq, head),
        P(seq, head),
        P(None, head),
        P(None, head),
        P(None, head),
        P(),
        P(seq, head),
    )
    return jax.shard_map(
        body, mesh=grid, in_specs=in_specs, out_specs=(P(seq, head),) * 5, check_vma=False
    )
```

```python
import functools
import math

import jax
import jax.numpy as jnp
from jax import lax
from jax.experimental import pallas as pl
from jax.experimental.pallas import tpu as pltpu
from jax.sharding import Mesh, PartitionSpec as P

HQ = 40
KVH = 8
HD = 128
L = 512
GROUP = HQ // KVH
WIDTH = GROUP * HD
FACTOR = HD ** (-0.5)
LOG_FACTOR = FACTOR * math.log2(math.e)
STATS = 16
SIDE = 4
LOW = -1e30
PLACES = (1, 3, 2)
Z = ("z_high", "z_low")
BF16 = jnp.bfloat16
F32 = jnp.float32


def dot_nt(a, b):
    return lax.dot_general(a, b, (((1,), (1,)), ((), ())), preferred_element_type=F32)


def dot_nn(a, b):
    return lax.dot_general(a, b, (((1,), (0,)), ((), ())), preferred_element_type=F32)


def head_lanes(head):
    return pl.ds(pl.multiple_of(head * HD, HD), HD)


def load_head(ref, head):
    return ref[:, :, head_lanes(head)].reshape(SIDE * HD, HD)


def load_own(ref, info):
    own = ref[info[0]]
    return jnp.concatenate([own[:, h * HD : (h + 1) * HD] for h in range(GROUP)], axis=0)


def own_lanes(row, info):
    pieces = [row[:, i * HD : (i + 1) * HD] for i in range(SIDE)]
    return sum(jnp.where(info[0] == i, piece, 0.0) for i, piece in enumerate(pieces))


def response_rows(info):
    return pl.ds(pl.multiple_of(info[0] * L, L), L)


def causal(info):
    keys = lax.broadcasted_iota(jnp.int32, (L, HD), 0)
    rows = lax.broadcasted_iota(jnp.int32, (L, HD), 1) + info[1] * HD
    return jnp.concatenate([keys <= rows] * GROUP, axis=1)


def local_stats(scores, dprods):
    top = jnp.max(scores, axis=0, keepdims=True)
    weights = jnp.exp2(scores - top)
    total = jnp.sum(weights, axis=0, keepdims=True)
    mixed = jnp.sum(weights * dprods, axis=0, keepdims=True)
    return top, total, mixed


def merge(found):
    top = functools.reduce(jnp.maximum, [item[0] for item in found])
    scales = [jnp.exp2(item[0] - top) for item in found]
    total = sum(item[1] * scale for item, scale in zip(found, scales))
    mixed = sum(item[2] * scale for item, scale in zip(found, scales))
    return top, total, mixed


def block_stats(q, g, keys, values):
    return local_stats(dot_nt(keys, q) * LOG_FACTOR, dot_nt(values, g))


def put_stats(ref, head, found):
    for kind in range(3):
        ref[pl.ds(kind * GROUP + head, 1), :] = found[kind]


def get_stats(ref, head):
    return tuple(ref[pl.ds(kind * GROUP + head, 1), :] for kind in range(3))


def own_stats_kernel(info, q_ref, g_ref, pair_ref, sk_ref, sv_ref, out_ref):
    out_ref[...] = jnp.zeros_like(out_ref)
    scores = dot_nt(sk_ref[response_rows(info), :], load_own(q_ref, info)) * LOG_FACTOR
    scores = jnp.where(causal(info), scores, -jnp.inf)
    own = local_stats(scores, dot_nt(sv_ref[response_rows(info), :], load_own(g_ref, info)))
    mine = lax.broadcasted_iota(jnp.int32, (1, SIDE * HD), 1) // HD == info[0]
    for head in range(GROUP):
        wide = [jnp.concatenate([item[:, head * HD : (head + 1) * HD]] * SIDE, axis=1) for item in own]
        put_stats(out_ref, head, [jnp.where(mine, a, b) for a, b in zip(wide, (LOW, 0.0, 0.0))])

    @pl.loop(0, GROUP)
    def _(head):
        found = block_stats(load_head(q_ref, head), load_head(g_ref, head), pair_ref[0], pair_ref[1])
        put_stats(out_ref, head, merge([found, get_stats(out_ref, head)]))


def rest_stats_kernel(info, q_ref, g_ref, p1_ref, p2_ref, p3_ref, former_ref, out_ref):
    out_ref[...] = jnp.zeros_like(out_ref)

    @pl.loop(0, GROUP)
    def _(head):
        q, g = load_head(q_ref, head), load_head(g_ref, head)
        found = [get_stats(former_ref, head)]
        for ref in (p1_ref, p2_ref, p3_ref):
            found.append(block_stats(q, g, ref[0], ref[1]))
        found = merge(found)
        for copy in range(SIDE):
            put_stats(out_ref.at[copy], head, found)


def score_grads(k, v, q, g, log_sum, delta, allowed=None):
    probs = jnp.exp2(dot_nt(k, q) * LOG_FACTOR - log_sum)
    if allowed is not None:
        probs = jnp.where(allowed, probs, 0.0)
    dscores = (probs * (dot_nt(v, g) - delta)).astype(BF16)
    return probs.astype(BF16), dscores


def grads_kernel(
    info, q_ref, g_ref, p0_ref, p1_ref, p2_ref, p3_ref, sk_ref, sv_ref, part_ref,
    dq0_ref, dq1_ref, dq2_ref, dq3_ref, own_ref, send1_ref, send2_ref, send3_ref,
    stat_ref, keyt_ref, dkey_ref, dvalue_ref, dself_key_ref, dself_value_ref, dself_query_ref, piece_ref,
):
    pair_refs = (p0_ref, p1_ref, p2_ref, p3_ref)
    parts = [
        tuple(part_ref[i, kind * GROUP : (kind + 1) * GROUP, :] for kind in range(3)) for i in range(SIDE)
    ]
    top, total, mixed = merge(parts)
    stat_ref[:GROUP, :] = top + jnp.log2(total)
    stat_ref[GROUP : 2 * GROUP, :] = mixed / total
    for i in range(SIDE):
        keyt_ref[i] = pair_refs[i][0].T
    dkey_ref[...] = jnp.zeros_like(dkey_ref)
    dvalue_ref[...] = jnp.zeros_like(dvalue_ref)

    q, g = load_own(q_ref, info), load_own(g_ref, info)
    keys = sk_ref[response_rows(info), :]
    log_sum, delta = (
        jnp.concatenate([own_lanes(stat_ref[first + h : first + h + 1, :], info) for h in range(GROUP)], axis=1)
        for first in (0, GROUP)
    )
    probs, dscores = score_grads(
        keys, sv_ref[response_rows(info), :], q, g, log_sum, delta, causal(info)
    )
    dself_value_ref[...] = dot_nn(probs, g)
    dself_key_ref[...] = dot_nn(dscores, q)
    dself_query_ref[...] = dot_nn(keys.T, dscores)

    @pl.loop(0, GROUP)
    def _(head):
        log_sum = stat_ref[pl.ds(head, 1), :]
        delta = stat_ref[pl.ds(GROUP + head, 1), :]
        q, g = load_head(q_ref, head), load_head(g_ref, head)
        dq = jnp.zeros((HD, SIDE * HD), F32)
        for i in range(SIDE):
            probs, dscores = score_grads(pair_refs[i][0], pair_refs[i][1], q, g, log_sum, delta)
            dvalue_ref[i] += dot_nn(probs, g)
            dkey_ref[i] += dot_nn(dscores, q)
            dq = dq + dot_nn(keyt_ref[i], dscores)
        own = dself_query_ref[:, head_lanes(head)]
        for response in range(SIDE):
            piece = dq[:, response * HD : (response + 1) * HD]
            piece = piece + jnp.where(response == info[0], own, 0.0)
            piece_ref[response] = (piece * FACTOR).T.astype(BF16)
        for step, out_ref in zip((0,) + PLACES, (dq0_ref, dq1_ref, dq2_ref, dq3_ref)):
            response = lax.rem(info[0] + step, SIDE)
            out_ref[0, :, head_lanes(head)] = piece_ref[response]
            out_ref[1, :, head_lanes(head)] = piece_ref[response ^ 1]

    for i, step, ref in zip(range(SIDE), (0,) + PLACES, (own_ref, send1_ref, send2_ref, send3_ref)):
        source = lax.rem(info[1] + SIDE - step, SIDE)
        slots = pl.ds(pl.multiple_of(source * HD, HD), HD)
        ref[:L, :HD] = (dkey_ref[i] * FACTOR).astype(ref.dtype)
        ref[:L, HD:] = dvalue_ref[i].astype(ref.dtype)
        ref[L:, :HD] = (dself_key_ref[slots, :] * FACTOR).astype(ref.dtype)
        ref[L:, HD:] = dself_value_ref[slots, :].astype(ref.dtype)


def finish_kernel(own_ref, b1_ref, b2_ref, b3_ref, dk_ref, dv_ref, dsk_ref, dsv_ref):
    total = own_ref[...] + sum(ref[...].astype(F32) for ref in (b1_ref, b2_ref, b3_ref))
    dk_ref[...] = total[:L, :HD]
    dv_ref[...] = total[:L, HD:]
    dsk_ref[...] = total[L:, :HD]
    dsv_ref[...] = total[L:, HD:]


def sum_turn_kernel(parts_ref, out_ref):
    total = parts_ref[0].astype(F32)
    for part in range(1, parts_ref.shape[0]):
        total = total + parts_ref[part].astype(F32)
    out_ref[...] = total.T.astype(BF16)


def project_blocks(info, weight_refs, core, rows, put):
    depth = weight_refs[0].shape[1]
    for step, weight_ref in zip((0,) + PLACES, weight_refs):
        source = lax.rem(info[1] + SIDE - step, SIDE)
        at = pl.ds(pl.multiple_of(lax.rem(source, 2) * depth, depth), depth)

        @pl.when(lax.div(source, 2) == core)
        def _():
            for block in range(2):
                terms = dot_nt(weight_ref[block], rows)
                for part in range(2):
                    put(part, block, at, terms[:, part * HD : (part + 1) * HD])


def project_theirs_kernel(
    info, d0_ref, d1_ref, d2_ref, d3_ref, w0_ref, w1_ref, w2_ref, w3_ref, out_ref, rows_ref
):
    for part in range(2):
        total = sum(ref[part].astype(F32) for ref in (d0_ref, d1_ref, d2_ref, d3_ref))
        rows_ref[part * HD : (part + 1) * HD, :] = total.astype(BF16)

    def put(part, block, at, terms):
        out_ref[part, block, at, :] = terms.astype(BF16)

    project_blocks(info, (w0_ref, w1_ref, w2_ref, w3_ref), 1 - info[2], rows_ref[...], put)


def project_mine_kernel(
    info, rows_ref, theirs_ref, w0_ref, w1_ref, w2_ref, w3_ref, out_ref
):
    columns = (info[0], SIDE - 1 - info[0])

    def put(part, block, at, terms):
        terms = terms + theirs_ref[part, block, at, :].astype(F32)
        out_ref[columns[block] ^ part, at, :] = terms.astype(BF16)

    project_blocks(info, (w0_ref, w1_ref, w2_ref, w3_ref), info[2], rows_ref[...], put)


def ring(step):
    return [(i, (i + step) % SIDE) for i in range(SIDE)]


def spread(array, axis):
    return [lax.ppermute(array, axis, ring(step)) for step in PLACES]


def body(queries, doc_keys, doc_values, self_keys, self_values, out_grads, lengths, query_weight):
    doc_rows = doc_keys.shape[0]
    place_y = lax.axis_index("y").astype(jnp.int32)
    info = jnp.stack([lax.axis_index(Z).astype(jnp.int32), place_y, lax.axis_index("core").astype(jnp.int32)])
    pair = jnp.stack([doc_keys, doc_values])
    pairs = [pair] + spread(pair, "y")
    other = lax.ppermute(query_weight, Z, [(i, SIDE - 1 - i) for i in range(SIDE)])

    def own_rows(array):
        return lax.dynamic_slice_in_dim(array.reshape(SIDE, L, WIDTH), place_y * HD, HD, 1)

    valid = (jnp.arange(HD, dtype=jnp.int32) + place_y * HD)[None, :] < lengths[:, None]
    q_own = own_rows(queries)
    g_own = own_rows(out_grads) * valid[..., None].astype(out_grads.dtype)

    smem = pl.BlockSpec(memory_space=pltpu.SMEM)
    vmem = pl.BlockSpec(memory_space=pltpu.VMEM)

    def call(kernel, shapes, operands, name, megabytes=8, scratch=()):
        return pl.pallas_call(
            kernel,
            in_specs=[smem if a is info else vmem for a in operands],
            out_specs=jax.tree.map(lambda _: vmem, shapes),
            out_shape=shapes,
            scratch_shapes=scratch,
            compiler_params=pltpu.CompilerParams(vmem_limit_bytes=megabytes * 1024 * 1024),
            name=name,
        )(*operands)

    shape = jax.ShapeDtypeStruct
    stats = call(
        own_stats_kernel,
        shape((STATS, SIDE * HD), F32),
        (info, q_own, g_own, pair, self_keys, self_values),
        "own_stats",
    )
    weight = jnp.stack([query_weight, other])
    weight, stats, *pairs = lax.optimization_barrier((weight, stats, *pairs))
    weights = [weight] + spread(weight, "y")
    stats = call(
        rest_stats_kernel,
        shape((SIDE, STATS, SIDE * HD), F32),
        (info, q_own, g_own, *pairs[1:], stats),
        "rest_stats",
    )
    parts = lax.all_to_all(stats, Z, 0, 0, tiled=True)

    grad_shape = shape((2, HD, WIDTH), BF16)
    back_shape = shape((doc_rows + HD, 2 * HD), BF16)
    found = call(
        grads_kernel,
        [grad_shape] * SIDE + [shape(back_shape.shape, F32)] + [back_shape] * 3,
        (info, q_own, g_own, *pairs, self_keys, self_values, parts),
        "local_grads",
        megabytes=14,
        scratch=[
            pltpu.VMEM((STATS, SIDE * HD), F32),
            pltpu.VMEM((SIDE, HD, doc_rows), BF16),
            pltpu.VMEM((SIDE, doc_rows, HD), F32),
            pltpu.VMEM((SIDE, doc_rows, HD), F32),
            pltpu.VMEM((L, HD), F32),
            pltpu.VMEM((L, HD), F32),
            pltpu.VMEM((HD, WIDTH), F32),
            pltpu.VMEM((SIDE, HD, HD), BF16),
        ],
    )
    dq, dq_sends, own, sends = found[0], found[1:SIDE], found[SIDE], found[SIDE + 1 :]
    dq_parts = [lax.ppermute(a, Z, ring(step)) for step, a in zip(PLACES, dq_sends)]
    weights, sends = lax.optimization_barrier((weights, sends))
    backs = [lax.ppermute(a, "y", ring(SIDE - step)) for step, a in zip(PLACES, sends)]
    dq_parts, backs[:2] = lax.optimization_barrier((dq_parts, backs[:2]))
    columns = 2 * query_weight.shape[0]
    theirs, rows = call(
        project_theirs_kernel,
        [shape((2, 2, columns, HD), BF16), shape((2 * HD, WIDTH), BF16)],
        (info, dq, *dq_parts, *weights),
        "project_theirs",
    )
    theirs = lax.ppermute(theirs, "core", [(0, 1), (1, 0)])
    terms = call(
        project_mine_kernel,
        shape((SIDE, columns, HD), BF16),
        (info, rows, theirs, *weights),
        "project_mine",
    )
    terms = lax.all_to_all(terms, "x", 0, 0, tiled=True)
    input_grads = call(sum_turn_kernel, shape((HD, columns), BF16), (terms,), "sum_groups")
    moves = []
    for z in range(SIDE):
        for x in range(SIDE):
            stays = x in (z, SIDE - 1 - z)
            moves.append((z * SIDE + x, z * SIDE + x if stays else (z ^ 1) * SIDE + (x ^ 1)))
    input_grads = lax.ppermute(input_grads, Z + ("x",), moves)
    grads = call(
        finish_kernel,
        [shape((doc_rows, HD), F32)] * 2 + [shape((HD, HD), F32)] * 2,
        (own, *backs),
        "sum_key_values",
    )
    return (input_grads, *grads)


def solution(mesh):
    names = ("z_high", "z_low", "y", "x", "core")
    grid = Mesh(mesh.devices.reshape(2, 2, SIDE, SIDE, 2), names)
    seq, head = names[:3], names[3:]
    in_specs = (
        P(None, head),
        P(seq, head),
        P(seq, head),
        P(None, head),
        P(None, head),
        P(None, head),
        P(),
        P(seq, head),
    )
    return jax.shard_map(
        body, mesh=grid, in_specs=in_specs, out_specs=(P(seq, head),) * 5, check_vma=False
    )
```

```python
import functools
import math

import jax
import jax.numpy as jnp
from jax import lax
from jax.experimental import pallas as pl
from jax.experimental.pallas import tpu as pltpu
from jax.sharding import Mesh, PartitionSpec as P

HQ = 40
KVH = 8
HD = 128
L = 512
GROUP = HQ // KVH
WIDTH = GROUP * HD
FACTOR = HD ** (-0.5)
LOG_FACTOR = FACTOR * math.log2(math.e)
STATS = 16
SIDE = 4
LOW = -1e30
HIGH = 1e30
PLACES = (1, 3, 2)
Z = ("z_high", "z_low")
BF16 = jnp.bfloat16
F32 = jnp.float32


def dot_nt(a, b):
    return lax.dot_general(a, b, (((1,), (1,)), ((), ())), preferred_element_type=F32)


def dot_nn(a, b):
    return lax.dot_general(a, b, (((1,), (0,)), ((), ())), preferred_element_type=F32)


def head_lanes(head):
    return pl.ds(pl.multiple_of(head * HD, HD), HD)


def load_head(ref, head):
    return ref[:, :, head_lanes(head)].reshape(SIDE * HD, HD)


def load_own(ref, info):
    own = ref[info[0]]
    return jnp.concatenate([own[:, h * HD : (h + 1) * HD] for h in range(GROUP)], axis=0)


def own_lanes(row, info):
    pieces = [row[:, i * HD : (i + 1) * HD] for i in range(SIDE)]
    return sum(jnp.where(info[0] == i, piece, 0.0) for i, piece in enumerate(pieces))


def response_rows(info):
    return pl.ds(pl.multiple_of(info[0] * L, L), L)


def causal(info):
    keys = lax.broadcasted_iota(jnp.int32, (L, HD), 0)
    rows = lax.broadcasted_iota(jnp.int32, (L, HD), 1) + info[1] * HD
    return jnp.concatenate([keys <= rows] * GROUP, axis=1)


def local_stats(scores, dprods):
    top = jnp.max(scores, axis=0, keepdims=True)
    weights = jnp.exp2(scores - top)
    total = jnp.sum(weights, axis=0, keepdims=True)
    mixed = jnp.sum(weights * dprods, axis=0, keepdims=True)
    return top, total, mixed


def merge(found):
    top = functools.reduce(jnp.maximum, [item[0] for item in found])
    scales = [jnp.exp2(item[0] - top) for item in found]
    total = sum(item[1] * scale for item, scale in zip(found, scales))
    mixed = sum(item[2] * scale for item, scale in zip(found, scales))
    return top, total, mixed


def block_stats(q, g, keys, values):
    return local_stats(dot_nt(keys, q) * LOG_FACTOR, dot_nt(values, g))


def put_stats(ref, head, found):
    for kind in range(3):
        ref[pl.ds(kind * GROUP + head, 1), :] = found[kind]


def get_stats(ref, head):
    return tuple(ref[pl.ds(kind * GROUP + head, 1), :] for kind in range(3))


def own_stats_kernel(info, q_ref, g_ref, pair_ref, sk_ref, sv_ref, out_ref):
    out_ref[...] = jnp.zeros_like(out_ref)
    scores = dot_nt(sk_ref[response_rows(info), :], load_own(q_ref, info)) * LOG_FACTOR
    scores = jnp.where(causal(info), scores, -jnp.inf)
    own = local_stats(scores, dot_nt(sv_ref[response_rows(info), :], load_own(g_ref, info)))
    mine = lax.broadcasted_iota(jnp.int32, (1, SIDE * HD), 1) // HD == info[0]
    for head in range(GROUP):
        wide = [jnp.concatenate([item[:, head * HD : (head + 1) * HD]] * SIDE, axis=1) for item in own]
        put_stats(out_ref, head, [jnp.where(mine, a, b) for a, b in zip(wide, (LOW, 0.0, 0.0))])

    @pl.loop(0, GROUP, unroll=True)
    def _(head):
        found = block_stats(load_head(q_ref, head), load_head(g_ref, head), pair_ref[0], pair_ref[1])
        put_stats(out_ref, head, merge([found, get_stats(out_ref, head)]))


def rest_stats_kernel(info, q_ref, g_ref, *refs):
    pair_refs, former_ref, out_ref = refs[:-2], refs[-2], refs[-1]
    wide = len(out_ref.shape) > 2

    def put(head, found):
        for copy in range(SIDE if wide else 1):
            put_stats(out_ref.at[copy] if wide else out_ref, head, found)

    out_ref[...] = jnp.zeros_like(out_ref)

    @pl.loop(0, GROUP, unroll=True)
    def _(head):
        q, g = load_head(q_ref, head), load_head(g_ref, head)
        top, total, mixed = get_stats(former_ref, head)
        for ref in pair_refs:
            weights = jnp.exp2(dot_nt(ref[0], q) * LOG_FACTOR - top)
            total = total + jnp.sum(weights, axis=0, keepdims=True)
            mixed = mixed + jnp.sum(weights * dot_nt(ref[1], g), axis=0, keepdims=True)
        put(head, (top, total, mixed))

    sums = (out_ref.at[0] if wide else out_ref)[GROUP : 2 * GROUP, :]

    @pl.when(jnp.logical_not(jnp.max(sums) < HIGH))
    def _():
        @pl.loop(0, GROUP)
        def _(head):
            q, g = load_head(q_ref, head), load_head(g_ref, head)
            found = [get_stats(former_ref, head)]
            for ref in pair_refs:
                found.append(block_stats(q, g, ref[0], ref[1]))
            put(head, merge(found))


def score_grads(k, v, q, g, log_sum, delta, allowed=None):
    probs = jnp.exp2(dot_nt(k, q) * LOG_FACTOR - log_sum)
    if allowed is not None:
        probs = jnp.where(allowed, probs, 0.0)
    dscores = (probs * (dot_nt(v, g) - delta)).astype(BF16)
    return probs.astype(BF16), dscores


def grads_kernel(
    info, q_ref, g_ref, p0_ref, p1_ref, p2_ref, p3_ref, sk_ref, sv_ref, part_ref,
    dq0_ref, dq1_ref, dq2_ref, dq3_ref, own_ref, send1_ref, send2_ref, send3_ref,
    stat_ref, keyt_ref, dkey_ref, dvalue_ref, dself_key_ref, dself_value_ref, dself_query_ref, piece_ref,
):
    pair_refs = (p0_ref, p1_ref, p2_ref, p3_ref)
    parts = [
        tuple(part_ref[i, kind * GROUP : (kind + 1) * GROUP, :] for kind in range(3)) for i in range(SIDE)
    ]
    top, total, mixed = merge(parts)
    stat_ref[:GROUP, :] = top + jnp.log2(total)
    stat_ref[GROUP : 2 * GROUP, :] = mixed / total
    for i in range(SIDE):
        keyt_ref[i] = pair_refs[i][0].T
    dkey_ref[...] = jnp.zeros_like(dkey_ref)
    dvalue_ref[...] = jnp.zeros_like(dvalue_ref)

    q, g = load_own(q_ref, info), load_own(g_ref, info)
    keys = sk_ref[response_rows(info), :]
    log_sum, delta = (
        jnp.concatenate([own_lanes(stat_ref[first + h : first + h + 1, :], info) for h in range(GROUP)], axis=1)
        for first in (0, GROUP)
    )
    probs, dscores = score_grads(
        keys, sv_ref[response_rows(info), :], q, g, log_sum, delta, causal(info)
    )
    dself_value_ref[...] = dot_nn(probs, g)
    dself_key_ref[...] = dot_nn(dscores, q)
    dself_query_ref[...] = dot_nn(keys.T, dscores)

    @pl.loop(0, GROUP, unroll=True)
    def _(head):
        log_sum = stat_ref[pl.ds(head, 1), :]
        delta = stat_ref[pl.ds(GROUP + head, 1), :]
        q, g = load_head(q_ref, head), load_head(g_ref, head)
        dq = jnp.zeros((HD, SIDE * HD), F32)
        for i in range(SIDE):
            probs, dscores = score_grads(pair_refs[i][0], pair_refs[i][1], q, g, log_sum, delta)
            dvalue_ref[i] += dot_nn(probs, g)
            dkey_ref[i] += dot_nn(dscores, q)
            dq = dq + dot_nn(keyt_ref[i], dscores)
        own = dself_query_ref[:, head_lanes(head)]
        for response in range(SIDE):
            piece = dq[:, response * HD : (response + 1) * HD]
            piece = piece + jnp.where(response == info[0], own, 0.0)
            piece_ref[response] = (piece * FACTOR).T.astype(BF16)
        for step, out_ref in zip((0,) + PLACES, (dq0_ref, dq1_ref, dq2_ref, dq3_ref)):
            response = lax.rem(info[0] + step, SIDE)
            out_ref[0, :, head_lanes(head)] = piece_ref[response]
            out_ref[1, :, head_lanes(head)] = piece_ref[response ^ 1]

    for i, step, ref in zip(range(SIDE), (0,) + PLACES, (own_ref, send1_ref, send2_ref, send3_ref)):
        source = lax.rem(info[1] + SIDE - step, SIDE)
        slots = pl.ds(pl.multiple_of(source * HD, HD), HD)
        ref[:L, :HD] = (dkey_ref[i] * FACTOR).astype(ref.dtype)
        ref[:L, HD:] = dvalue_ref[i].astype(ref.dtype)
        ref[L:, :HD] = (dself_key_ref[slots, :] * FACTOR).astype(ref.dtype)
        ref[L:, HD:] = dself_value_ref[slots, :].astype(ref.dtype)


def finish_kernel(own_ref, b1_ref, b2_ref, b3_ref, dk_ref, dv_ref, dsk_ref, dsv_ref):
    total = own_ref[...] + sum(ref[...].astype(F32) for ref in (b1_ref, b2_ref, b3_ref))
    dk_ref[...] = total[:L, :HD]
    dv_ref[...] = total[:L, HD:]
    dsk_ref[...] = total[L:, :HD]
    dsv_ref[...] = total[L:, HD:]


def sum_turn_kernel(a_ref, b_ref, c_ref, d_ref, out_ref):
    total = sum(ref[...].astype(F32) for ref in (a_ref, b_ref, c_ref, d_ref))
    out_ref[...] = total.T.astype(BF16)


def project_blocks(info, weight_refs, core, rows, put):
    depth = weight_refs[0].shape[1]
    for step, weight_ref in zip((0,) + PLACES, weight_refs):
        source = lax.rem(info[1] + SIDE - step, SIDE)
        at = pl.ds(pl.multiple_of(lax.rem(source, 2) * depth, depth), depth)

        @pl.when(lax.div(source, 2) == core)
        def _():
            for block in range(2):
                terms = dot_nt(weight_ref[block], rows)
                for part in range(2):
                    put(part, block, at, terms[:, part * HD : (part + 1) * HD])


def project_theirs_kernel(
    info, d0_ref, d1_ref, d2_ref, d3_ref, w0_ref, w1_ref, w2_ref, w3_ref, out_ref, rows_ref
):
    for part in range(2):
        total = sum(ref[part].astype(F32) for ref in (d0_ref, d1_ref, d2_ref, d3_ref))
        rows_ref[part * HD : (part + 1) * HD, :] = total.astype(BF16)

    def put(part, block, at, terms):
        out_ref[part, block, at, :] = terms.astype(BF16)

    project_blocks(info, (w0_ref, w1_ref, w2_ref, w3_ref), 1 - info[2], rows_ref[...], put)


def project_mine_kernel(
    info, rows_ref, theirs_ref, w0_ref, w1_ref, w2_ref, w3_ref, o0_ref, o1_ref, o2_ref, o3_ref, out_ref
):
    columns = (info[0], SIDE - 1 - info[0])

    def put(part, block, at, terms):
        terms = terms + theirs_ref[part, block, at, :].astype(F32)
        out_ref[columns[block] ^ part, at, :] = terms.astype(BF16)

    project_blocks(info, (w0_ref, w1_ref, w2_ref, w3_ref), info[2], rows_ref[...], put)
    for step, ref in zip((0,) + PLACES, (o0_ref, o1_ref, o2_ref, o3_ref)):
        ref[...] = out_ref[lax.rem(info[3] + step, SIDE)]


def ring(step):
    return [(i, (i + step) % SIDE) for i in range(SIDE)]


def spread(array, axis):
    return [lax.ppermute(array, axis, ring(step)) for step in PLACES]


def body(queries, doc_keys, doc_values, self_keys, self_values, out_grads, lengths, query_weight):
    doc_rows = doc_keys.shape[0]
    place_y = lax.axis_index("y").astype(jnp.int32)
    info = jnp.stack([lax.axis_index(Z).astype(jnp.int32), place_y, lax.axis_index("core").astype(jnp.int32), lax.axis_index("x").astype(jnp.int32)])
    pair = jnp.stack([doc_keys, doc_values])
    pairs = [pair] + spread(pair, "y")
    other = lax.ppermute(query_weight, Z, [(i, SIDE - 1 - i) for i in range(SIDE)])

    def own_rows(array):
        return lax.dynamic_slice_in_dim(array.reshape(SIDE, L, WIDTH), place_y * HD, HD, 1)

    valid = (jnp.arange(HD, dtype=jnp.int32) + place_y * HD)[None, :] < lengths[:, None]
    q_own = own_rows(queries)
    g_own = own_rows(out_grads) * valid[..., None].astype(out_grads.dtype)

    smem = pl.BlockSpec(memory_space=pltpu.SMEM)
    vmem = pl.BlockSpec(memory_space=pltpu.VMEM)

    def call(kernel, shapes, operands, name, megabytes=8, scratch=()):
        return pl.pallas_call(
            kernel,
            in_specs=[smem if a is info else vmem for a in operands],
            out_specs=jax.tree.map(lambda _: vmem, shapes),
            out_shape=shapes,
            scratch_shapes=scratch,
            compiler_params=pltpu.CompilerParams(vmem_limit_bytes=megabytes * 1024 * 1024),
            name=name,
        )(*operands)

    shape = jax.ShapeDtypeStruct
    stats = call(
        own_stats_kernel,
        shape((STATS, SIDE * HD), F32),
        (info, q_own, g_own, pair, self_keys, self_values),
        "own_stats",
    )
    weight = jnp.stack([query_weight, other])
    weight, stats, *pairs = lax.optimization_barrier((weight, stats, *pairs))
    weights = [weight] + spread(weight, "y")
    stats = call(
        rest_stats_kernel,
        shape((SIDE, STATS, SIDE * HD), F32),
        (info, q_own, g_own, *pairs[1:], stats),
        "rest_stats",
    )
    parts = lax.all_to_all(stats, Z, 0, 0, tiled=True)

    grad_shape = shape((2, HD, WIDTH), BF16)
    back_shape = shape((doc_rows + HD, 2 * HD), BF16)
    found = call(
        grads_kernel,
        [grad_shape] * SIDE + [shape(back_shape.shape, F32)] + [back_shape] * 3,
        (info, q_own, g_own, *pairs, self_keys, self_values, parts),
        "local_grads",
        megabytes=14,
        scratch=[
            pltpu.VMEM((STATS, SIDE * HD), F32),
            pltpu.VMEM((SIDE, HD, doc_rows), BF16),
            pltpu.VMEM((SIDE, doc_rows, HD), F32),
            pltpu.VMEM((SIDE, doc_rows, HD), F32),
            pltpu.VMEM((L, HD), F32),
            pltpu.VMEM((L, HD), F32),
            pltpu.VMEM((HD, WIDTH), F32),
            pltpu.VMEM((SIDE, HD, HD), BF16),
        ],
    )
    dq, dq_sends, own, sends = found[0], found[1:SIDE], found[SIDE], found[SIDE + 1 :]
    dq_parts = [lax.ppermute(a, Z, ring(step)) for step, a in zip(PLACES, dq_sends)]
    weights, sends = lax.optimization_barrier((weights, sends))
    backs = [lax.ppermute(a, "y", ring(SIDE - step)) for step, a in zip(PLACES, sends)]
    dq_parts, backs[:2] = lax.optimization_barrier((dq_parts, backs[:2]))
    columns = 2 * query_weight.shape[0]
    theirs, rows = call(
        project_theirs_kernel,
        [shape((2, 2, columns, HD), BF16), shape((2 * HD, WIDTH), BF16)],
        (info, dq, *dq_parts, *weights),
        "project_theirs",
    )
    theirs = lax.ppermute(theirs, "core", [(0, 1), (1, 0)])
    term, *terms = call(
        project_mine_kernel,
        [shape((columns, HD), BF16)] * SIDE,
        (info, rows, theirs, *weights),
        "project_mine",
        scratch=[pltpu.VMEM((SIDE, columns, HD), BF16)],
    )
    terms = [lax.ppermute(a, "x", ring(step)) for step, a in zip(PLACES, terms)]
    input_grads = call(sum_turn_kernel, shape((HD, columns), BF16), (term, *terms), "sum_groups")
    moves = []
    for z in range(SIDE):
        for x in range(SIDE):
            stays = x in (z, SIDE - 1 - z)
            moves.append((z * SIDE + x, z * SIDE + x if stays else (z ^ 1) * SIDE + (x ^ 1)))
    input_grads = lax.ppermute(input_grads, Z + ("x",), moves)
    grads = call(
        finish_kernel,
        [shape((doc_rows, HD), F32)] * 2 + [shape((HD, HD), F32)] * 2,
        (own, *backs),
        "sum_key_values",
    )
    return (input_grads, *grads)


def solution(mesh):
    names = ("z_high", "z_low", "y", "x", "core")
    grid = Mesh(mesh.devices.reshape(2, 2, SIDE, SIDE, 2), names)
    seq, head = names[:3], names[3:]
    in_specs = (
        P(None, head),
        P(seq, head),
        P(seq, head),
        P(None, head),
        P(None, head),
        P(None, head),
        P(),
        P(seq, head),
    )
    return jax.shard_map(
        body, mesh=grid, in_specs=in_specs, out_specs=(P(seq, head),) * 5, check_vma=False
    )
```

```python
import functools
import math

import jax
import jax.numpy as jnp
from jax import lax
from jax.experimental import pallas as pl
from jax.experimental.pallas import tpu as pltpu
from jax.sharding import Mesh, PartitionSpec as P

HQ = 40
KVH = 8
HD = 128
L = 512
GROUP = HQ // KVH
WIDTH = GROUP * HD
FACTOR = HD ** (-0.5)
LOG_FACTOR = FACTOR * math.log2(math.e)
STATS = 16
SIDE = 4
LOW = -1e30
HIGH = 1e30
PLACES = (1, 3, 2)
Z = ("z_high", "z_low")
BF16 = jnp.bfloat16
F32 = jnp.float32


def dot_nt(a, b):
    return lax.dot_general(a, b, (((1,), (1,)), ((), ())), preferred_element_type=F32)


def dot_nn(a, b):
    return lax.dot_general(a, b, (((1,), (0,)), ((), ())), preferred_element_type=F32)


def head_lanes(head):
    return pl.ds(pl.multiple_of(head * HD, HD), HD)


def load_head(ref, head):
    return ref[:, :, head_lanes(head)].reshape(SIDE * HD, HD)


def load_own(ref, info):
    own = ref[info[0]]
    return jnp.concatenate([own[:, h * HD : (h + 1) * HD] for h in range(GROUP)], axis=0)


def own_lanes(row, info):
    pieces = [row[:, i * HD : (i + 1) * HD] for i in range(SIDE)]
    return sum(jnp.where(info[0] == i, piece, 0.0) for i, piece in enumerate(pieces))


def response_rows(info):
    return pl.ds(pl.multiple_of(info[0] * L, L), L)


def causal(info):
    keys = lax.broadcasted_iota(jnp.int32, (L, HD), 0)
    rows = lax.broadcasted_iota(jnp.int32, (L, HD), 1) + info[1] * HD
    return jnp.concatenate([keys <= rows] * GROUP, axis=1)


def local_stats(scores, dprods):
    top = jnp.max(scores, axis=0, keepdims=True)
    weights = jnp.exp2(scores - top)
    total = jnp.sum(weights, axis=0, keepdims=True)
    mixed = jnp.sum(weights * dprods, axis=0, keepdims=True)
    return top, total, mixed


def merge(found):
    top = functools.reduce(jnp.maximum, [item[0] for item in found])
    scales = [jnp.exp2(item[0] - top) for item in found]
    total = sum(item[1] * scale for item, scale in zip(found, scales))
    mixed = sum(item[2] * scale for item, scale in zip(found, scales))
    return top, total, mixed


def block_stats(q, g, keys, values):
    return local_stats(dot_nt(keys, q) * LOG_FACTOR, dot_nt(values, g))


def put_stats(ref, head, found):
    for kind in range(3):
        ref[pl.ds(kind * GROUP + head, 1), :] = found[kind]


def get_stats(ref, head):
    return tuple(ref[pl.ds(kind * GROUP + head, 1), :] for kind in range(3))


def own_stats_kernel(info, q_ref, g_ref, pair_ref, sk_ref, sv_ref, out_ref):
    out_ref[...] = jnp.zeros_like(out_ref)
    scores = dot_nt(sk_ref[response_rows(info), :], load_own(q_ref, info)) * LOG_FACTOR
    scores = jnp.where(causal(info), scores, -jnp.inf)
    own = local_stats(scores, dot_nt(sv_ref[response_rows(info), :], load_own(g_ref, info)))
    mine = lax.broadcasted_iota(jnp.int32, (1, SIDE * HD), 1) // HD == info[0]
    for head in range(GROUP):
        wide = [jnp.concatenate([item[:, head * HD : (head + 1) * HD]] * SIDE, axis=1) for item in own]
        put_stats(out_ref, head, [jnp.where(mine, a, b) for a, b in zip(wide, (LOW, 0.0, 0.0))])

    @pl.loop(0, GROUP, unroll=True)
    def _(head):
        found = block_stats(load_head(q_ref, head), load_head(g_ref, head), pair_ref[0], pair_ref[1])
        put_stats(out_ref, head, merge([found, get_stats(out_ref, head)]))


def rest_stats_kernel(info, q_ref, g_ref, *refs):
    pair_refs, former_ref, out_ref = refs[:-2], refs[-2], refs[-1]
    wide = len(out_ref.shape) > 2

    def put(head, found):
        for copy in range(SIDE if wide else 1):
            put_stats(out_ref.at[copy] if wide else out_ref, head, found)

    out_ref[...] = jnp.zeros_like(out_ref)

    @pl.loop(0, GROUP, unroll=True)
    def _(head):
        q, g = load_head(q_ref, head), load_head(g_ref, head)
        top, total, mixed = get_stats(former_ref, head)
        for ref in pair_refs:
            weights = jnp.exp2(dot_nt(ref[0], q) * LOG_FACTOR - top)
            total = total + jnp.sum(weights, axis=0, keepdims=True)
            mixed = mixed + jnp.sum(weights * dot_nt(ref[1], g), axis=0, keepdims=True)
        put(head, (top, total, mixed))

    sums = (out_ref.at[0] if wide else out_ref)[GROUP : 2 * GROUP, :]

    @pl.when(jnp.logical_not(jnp.max(sums) < HIGH))
    def _():
        @pl.loop(0, GROUP)
        def _(head):
            q, g = load_head(q_ref, head), load_head(g_ref, head)
            found = [get_stats(former_ref, head)]
            for ref in pair_refs:
                found.append(block_stats(q, g, ref[0], ref[1]))
            put(head, merge(found))


def score_grads(k, v, q, g, log_sum, delta, allowed=None):
    probs = jnp.exp2(dot_nt(k, q) * LOG_FACTOR - log_sum)
    if allowed is not None:
        probs = jnp.where(allowed, probs, 0.0)
    dscores = (probs * (dot_nt(v, g) - delta)).astype(BF16)
    return probs.astype(BF16), dscores


def grads_kernel(
    info, q_ref, g_ref, p0_ref, p1_ref, p2_ref, p3_ref, sk_ref, sv_ref, part_ref,
    dq0_ref, dq1_ref, dq2_ref, dq3_ref, dkey_ref, dvalue_ref, dself_key_ref, dself_value_ref,
    stat_ref, keyt_ref, dself_query_ref, piece_ref,
):
    pair_refs = (p0_ref, p1_ref, p2_ref, p3_ref)
    parts = [
        tuple(part_ref[i, kind * GROUP : (kind + 1) * GROUP, :] for kind in range(3)) for i in range(SIDE)
    ]
    top, total, mixed = merge(parts)
    stat_ref[:GROUP, :] = top + jnp.log2(total)
    stat_ref[GROUP : 2 * GROUP, :] = mixed / total
    for i in range(SIDE):
        keyt_ref[i] = pair_refs[i][0].T

    q, g = load_own(q_ref, info), load_own(g_ref, info)
    keys = sk_ref[response_rows(info), :]
    log_sum, delta = (
        jnp.concatenate([own_lanes(stat_ref[first + h : first + h + 1, :], info) for h in range(GROUP)], axis=1)
        for first in (0, GROUP)
    )
    probs, dscores = score_grads(
        keys, sv_ref[response_rows(info), :], q, g, log_sum, delta, causal(info)
    )
    dself_value_ref[...] = dot_nn(probs, g)
    dself_key_ref[...] = dot_nn(dscores, q)
    dself_query_ref[...] = dot_nn(keys.T, dscores)

    for head in range(GROUP):
        log_sum = stat_ref[pl.ds(head, 1), :]
        delta = stat_ref[pl.ds(GROUP + head, 1), :]
        q, g = load_head(q_ref, head), load_head(g_ref, head)
        dq = jnp.zeros((HD, SIDE * HD), F32)
        for i in range(SIDE):
            probs, dscores = score_grads(pair_refs[i][0], pair_refs[i][1], q, g, log_sum, delta)
            dvalue, dkey = dot_nn(probs, g), dot_nn(dscores, q)
            dvalue_ref[i] = dvalue if head == 0 else dvalue_ref[i] + dvalue
            dkey_ref[i] = dkey if head == 0 else dkey_ref[i] + dkey
            dq = dq + dot_nn(keyt_ref[i], dscores)
        own = dself_query_ref[:, head_lanes(head)]
        for response in range(SIDE):
            piece = dq[:, response * HD : (response + 1) * HD]
            piece = piece + jnp.where(response == info[0], own, 0.0)
            piece_ref[response] = (piece * FACTOR).T.astype(BF16)
        for step, out_ref in zip((0,) + PLACES, (dq0_ref, dq1_ref, dq2_ref, dq3_ref)):
            response = lax.rem(info[0] + step, SIDE)
            out_ref[0, :, head_lanes(head)] = piece_ref[response]
            out_ref[1, :, head_lanes(head)] = piece_ref[response ^ 1]


def split_kernel(
    info, dkey_ref, dvalue_ref, dself_key_ref, dself_value_ref, own_ref, send1_ref, send2_ref, send3_ref
):
    for i, step, ref in zip(range(SIDE), (0,) + PLACES, (own_ref, send1_ref, send2_ref, send3_ref)):
        source = lax.rem(info[1] + SIDE - step, SIDE)
        slots = pl.ds(pl.multiple_of(source * HD, HD), HD)
        ref[:L, :HD] = (dkey_ref[i] * FACTOR).astype(ref.dtype)
        ref[:L, HD:] = dvalue_ref[i].astype(ref.dtype)
        ref[L:, :HD] = (dself_key_ref[slots, :] * FACTOR).astype(ref.dtype)
        ref[L:, HD:] = dself_value_ref[slots, :].astype(ref.dtype)


def finish_kernel(own_ref, b1_ref, b2_ref, b3_ref, dk_ref, dv_ref, dsk_ref, dsv_ref):
    total = own_ref[...] + sum(ref[...].astype(F32) for ref in (b1_ref, b2_ref, b3_ref))
    dk_ref[...] = total[:L, :HD]
    dv_ref[...] = total[:L, HD:]
    dsk_ref[...] = total[L:, :HD]
    dsv_ref[...] = total[L:, HD:]


def sum_turn_kernel(a_ref, b_ref, c_ref, d_ref, out_ref):
    total = sum(ref[...].astype(F32) for ref in (a_ref, b_ref, c_ref, d_ref))
    out_ref[...] = total.T.astype(BF16)


def project_blocks(info, weight_refs, core, rows, put):
    depth = weight_refs[0].shape[1]
    for step, weight_ref in zip((0,) + PLACES, weight_refs):
        source = lax.rem(info[1] + SIDE - step, SIDE)
        at = pl.ds(pl.multiple_of(lax.rem(source, 2) * depth, depth), depth)

        @pl.when(lax.div(source, 2) == core)
        def _():
            for block in range(2):
                terms = dot_nt(weight_ref[block], rows)
                for part in range(2):
                    put(part, block, at, terms[:, part * HD : (part + 1) * HD])


def project_theirs_kernel(
    info, d0_ref, d1_ref, d2_ref, d3_ref, w0_ref, w1_ref, w2_ref, w3_ref, out_ref, rows_ref
):
    for part in range(2):
        total = sum(ref[part].astype(F32) for ref in (d0_ref, d1_ref, d2_ref, d3_ref))
        rows_ref[part * HD : (part + 1) * HD, :] = total.astype(BF16)

    def put(part, block, at, terms):
        out_ref[part, block, at, :] = terms.astype(BF16)

    project_blocks(info, (w0_ref, w1_ref, w2_ref, w3_ref), 1 - info[2], rows_ref[...], put)


def project_mine_kernel(
    info, rows_ref, theirs_ref, w0_ref, w1_ref, w2_ref, w3_ref, o0_ref, o1_ref, o2_ref, o3_ref, out_ref
):
    columns = (info[0], SIDE - 1 - info[0])

    def put(part, block, at, terms):
        terms = terms + theirs_ref[part, block, at, :].astype(F32)
        out_ref[columns[block] ^ part, at, :] = terms.astype(BF16)

    project_blocks(info, (w0_ref, w1_ref, w2_ref, w3_ref), info[2], rows_ref[...], put)
    for step, ref in zip((0,) + PLACES, (o0_ref, o1_ref, o2_ref, o3_ref)):
        ref[...] = out_ref[lax.rem(info[3] + step, SIDE)]


def ring(step):
    return [(i, (i + step) % SIDE) for i in range(SIDE)]


def spread(array, axis):
    return [lax.ppermute(array, axis, ring(step)) for step in PLACES]


def body(queries, doc_keys, doc_values, self_keys, self_values, out_grads, lengths, query_weight):
    doc_rows = doc_keys.shape[0]
    place_y = lax.axis_index("y").astype(jnp.int32)
    info = jnp.stack([lax.axis_index(Z).astype(jnp.int32), place_y, lax.axis_index("core").astype(jnp.int32), lax.axis_index("x").astype(jnp.int32)])
    pair = jnp.stack([doc_keys, doc_values])
    pairs = [pair] + [lax.ppermute(pair, "y", ring(step)) for step in PLACES[:2]]
    other = lax.ppermute(query_weight, Z, [(i, SIDE - 1 - i) for i in range(SIDE)])

    def own_rows(array):
        return lax.dynamic_slice_in_dim(array.reshape(SIDE, L, WIDTH), place_y * HD, HD, 1)

    valid = (jnp.arange(HD, dtype=jnp.int32) + place_y * HD)[None, :] < lengths[:, None]
    far, valid = lax.optimization_barrier((pair, valid))
    pairs.append(lax.ppermute(far, "y", ring(PLACES[2])))
    q_own = own_rows(queries)
    g_own = own_rows(out_grads) * valid[..., None].astype(out_grads.dtype)

    smem = pl.BlockSpec(memory_space=pltpu.SMEM)
    vmem = pl.BlockSpec(memory_space=pltpu.VMEM)

    def call(kernel, shapes, operands, name, megabytes=8, scratch=()):
        return pl.pallas_call(
            kernel,
            in_specs=[smem if a is info else vmem for a in operands],
            out_specs=jax.tree.map(lambda _: vmem, shapes),
            out_shape=shapes,
            scratch_shapes=scratch,
            compiler_params=pltpu.CompilerParams(vmem_limit_bytes=megabytes * 1024 * 1024),
            name=name,
        )(*operands)

    shape = jax.ShapeDtypeStruct
    stats = call(
        own_stats_kernel,
        shape((STATS, SIDE * HD), F32),
        (info, q_own, g_own, pair, self_keys, self_values),
        "own_stats",
    )
    weight = jnp.stack([query_weight, other])
    stats = call(
        rest_stats_kernel,
        shape((STATS, SIDE * HD), F32),
        (info, q_own, g_own, *pairs[1:3], stats),
        "near_stats",
    )
    weight, stats, pairs[3] = lax.optimization_barrier((weight, stats, pairs[3]))
    weights = [weight] + spread(weight, "y")
    stats = call(
        rest_stats_kernel,
        shape((SIDE, STATS, SIDE * HD), F32),
        (info, q_own, g_own, pairs[3], stats),
        "far_stats",
    )
    parts = lax.all_to_all(stats, Z, 0, 0, tiled=True)

    grad_shape = shape((2, HD, WIDTH), BF16)
    back_shape = shape((doc_rows + HD, 2 * HD), BF16)
    found = call(
        grads_kernel,
        [grad_shape] * SIDE + [shape((SIDE, doc_rows, HD), F32)] * 2 + [shape((L, HD), F32)] * 2,
        (info, q_own, g_own, *pairs, self_keys, self_values, parts),
        "local_grads",
        megabytes=14,
        scratch=[
            pltpu.VMEM((STATS, SIDE * HD), F32),
            pltpu.VMEM((SIDE, HD, doc_rows), BF16),
            pltpu.VMEM((HD, WIDTH), F32),
            pltpu.VMEM((SIDE, HD, HD), BF16),
        ],
    )
    dq, dq_sends = found[0], found[1:SIDE]
    own, *sends = call(
        split_kernel,
        [shape(back_shape.shape, F32)] + [back_shape] * 3,
        (info, *found[SIDE:]),
        "split_grads",
    )
    dq_parts = [lax.ppermute(a, Z, ring(step)) for step, a in zip(PLACES, dq_sends)]
    weights, sends = lax.optimization_barrier((weights, sends))
    backs = [lax.ppermute(a, "y", ring(SIDE - step)) for step, a in zip(PLACES, sends)]
    columns = 2 * query_weight.shape[0]
    theirs, rows = call(
        project_theirs_kernel,
        [shape((2, 2, columns, HD), BF16), shape((2 * HD, WIDTH), BF16)],
        (info, dq, *dq_parts, *weights),
        "project_theirs",
    )
    theirs = lax.ppermute(theirs, "core", [(0, 1), (1, 0)])
    term, *terms = call(
        project_mine_kernel,
        [shape((columns, HD), BF16)] * SIDE,
        (info, rows, theirs, *weights),
        "project_mine",
        scratch=[pltpu.VMEM((SIDE, columns, HD), BF16)],
    )
    terms = [lax.ppermute(a, "x", ring(step)) for step, a in zip(PLACES, terms)]
    terms, backs[:2] = lax.optimization_barrier((terms, backs[:2]))
    input_grads = call(sum_turn_kernel, shape((HD, columns), BF16), (term, *terms), "sum_groups")
    moves = []
    for z in range(SIDE):
        for x in range(SIDE):
            stays = x in (z, SIDE - 1 - z)
            moves.append((z * SIDE + x, z * SIDE + x if stays else (z ^ 1) * SIDE + (x ^ 1)))
    input_grads = lax.ppermute(input_grads, Z + ("x",), moves)
    grads = call(
        finish_kernel,
        [shape((doc_rows, HD), F32)] * 2 + [shape((HD, HD), F32)] * 2,
        (own, *backs),
        "sum_key_values",
    )
    return (input_grads, *grads)


def solution(mesh):
    names = ("z_high", "z_low", "y", "x", "core")
    grid = Mesh(mesh.devices.reshape(2, 2, SIDE, SIDE, 2), names)
    seq, head = names[:3], names[3:]
    in_specs = (
        P(None, head),
        P(seq, head),
        P(seq, head),
        P(None, head),
        P(None, head),
        P(None, head),
        P(),
        P(seq, head),
    )
    return jax.shard_map(
        body, mesh=grid, in_specs=in_specs, out_specs=(P(seq, head),) * 5, check_vma=False
    )
```

```python
import functools
import math

import jax
import jax.numpy as jnp
from jax import lax
from jax.experimental import pallas as pl
from jax.experimental.pallas import tpu as pltpu
from jax.sharding import Mesh, PartitionSpec as P

HQ = 40
KVH = 8
HD = 128
L = 512
GROUP = HQ // KVH
WIDTH = GROUP * HD
FACTOR = HD ** (-0.5)
LOG_FACTOR = FACTOR * math.log2(math.e)
STATS = 16
SIDE = 4
LOW = -1e30
HIGH = 1e30
PLACES = (1, 3, 2)
Z = ("z_high", "z_low")
BF16 = jnp.bfloat16
F32 = jnp.float32


def dot_nt(a, b):
    return lax.dot_general(a, b, (((1,), (1,)), ((), ())), preferred_element_type=F32)


def dot_nn(a, b):
    return lax.dot_general(a, b, (((1,), (0,)), ((), ())), preferred_element_type=F32)


def head_lanes(head):
    return pl.ds(pl.multiple_of(head * HD, HD), HD)


def load_head(ref, head):
    return ref[:, :, head_lanes(head)].reshape(SIDE * HD, HD)


def load_own(ref, info):
    own = ref[info[0]]
    return jnp.concatenate([own[:, h * HD : (h + 1) * HD] for h in range(GROUP)], axis=0)


def own_lanes(row, info):
    pieces = [row[:, i * HD : (i + 1) * HD] for i in range(SIDE)]
    return sum(jnp.where(info[0] == i, piece, 0.0) for i, piece in enumerate(pieces))


def response_rows(info):
    return pl.ds(pl.multiple_of(info[0] * L, L), L)


def causal(info):
    keys = lax.broadcasted_iota(jnp.int32, (L, HD), 0)
    rows = lax.broadcasted_iota(jnp.int32, (L, HD), 1) + info[1] * HD
    return jnp.concatenate([keys <= rows] * GROUP, axis=1)


def local_stats(scores, dprods):
    top = jnp.max(scores, axis=0, keepdims=True)
    weights = jnp.exp2(scores - top)
    total = jnp.sum(weights, axis=0, keepdims=True)
    mixed = jnp.sum(weights * dprods, axis=0, keepdims=True)
    return top, total, mixed


def merge(found):
    top = functools.reduce(jnp.maximum, [item[0] for item in found])
    scales = [jnp.exp2(item[0] - top) for item in found]
    total = sum(item[1] * scale for item, scale in zip(found, scales))
    mixed = sum(item[2] * scale for item, scale in zip(found, scales))
    return top, total, mixed


def block_stats(q, g, keys, values):
    return local_stats(dot_nt(keys, q) * LOG_FACTOR, dot_nt(values, g))


def put_stats(ref, head, found):
    for kind in range(3):
        ref[pl.ds(kind * GROUP + head, 1), :] = found[kind]


def get_stats(ref, head):
    return tuple(ref[pl.ds(kind * GROUP + head, 1), :] for kind in range(3))


def own_stats_kernel(info, q_ref, g_ref, pair_ref, sk_ref, sv_ref, out_ref):
    out_ref[...] = jnp.zeros_like(out_ref)
    scores = dot_nt(sk_ref[response_rows(info), :], load_own(q_ref, info)) * LOG_FACTOR
    scores = jnp.where(causal(info), scores, -jnp.inf)
    own = local_stats(scores, dot_nt(sv_ref[response_rows(info), :], load_own(g_ref, info)))
    mine = lax.broadcasted_iota(jnp.int32, (1, SIDE * HD), 1) // HD == info[0]
    for head in range(GROUP):
        wide = [jnp.concatenate([item[:, head * HD : (head + 1) * HD]] * SIDE, axis=1) for item in own]
        put_stats(out_ref, head, [jnp.where(mine, a, b) for a, b in zip(wide, (LOW, 0.0, 0.0))])

    @pl.loop(0, GROUP, unroll=True)
    def _(head):
        found = block_stats(load_head(q_ref, head), load_head(g_ref, head), pair_ref[0], pair_ref[1])
        put_stats(out_ref, head, merge([found, get_stats(out_ref, head)]))


def rest_stats_kernel(info, q_ref, g_ref, *refs):
    pair_refs, former_ref, out_ref = refs[:-2], refs[-2], refs[-1]
    wide = len(out_ref.shape) > 2

    def put(head, found):
        for copy in range(SIDE if wide else 1):
            put_stats(out_ref.at[copy] if wide else out_ref, head, found)

    out_ref[...] = jnp.zeros_like(out_ref)

    @pl.loop(0, GROUP, unroll=True)
    def _(head):
        q, g = load_head(q_ref, head), load_head(g_ref, head)
        top, total, mixed = get_stats(former_ref, head)
        for ref in pair_refs:
            weights = jnp.exp2(dot_nt(ref[0], q) * LOG_FACTOR - top)
            total = total + jnp.sum(weights, axis=0, keepdims=True)
            mixed = mixed + jnp.sum(weights * dot_nt(ref[1], g), axis=0, keepdims=True)
        put(head, (top, total, mixed))

    sums = (out_ref.at[0] if wide else out_ref)[GROUP : 2 * GROUP, :]

    @pl.when(jnp.logical_not(jnp.max(sums) < HIGH))
    def _():
        @pl.loop(0, GROUP)
        def _(head):
            q, g = load_head(q_ref, head), load_head(g_ref, head)
            found = [get_stats(former_ref, head)]
            for ref in pair_refs:
                found.append(block_stats(q, g, ref[0], ref[1]))
            put(head, merge(found))


def score_grads(k, v, q, g, log_sum, delta, allowed=None):
    probs = jnp.exp2(dot_nt(k, q) * LOG_FACTOR - log_sum)
    if allowed is not None:
        probs = jnp.where(allowed, probs, 0.0)
    dscores = (probs * (dot_nt(v, g) - delta)).astype(BF16)
    return probs.astype(BF16), dscores


def grads_kernel(
    info, q_ref, g_ref, p0_ref, p1_ref, p2_ref, p3_ref, sk_ref, sv_ref, part_ref,
    dq0_ref, dq1_ref, dq2_ref, dq3_ref, dkey_ref, dvalue_ref, dself_key_ref, dself_value_ref,
    stat_ref, keyt_ref, dself_query_ref, piece_ref,
):
    pair_refs = (p0_ref, p1_ref, p2_ref, p3_ref)
    parts = [
        tuple(part_ref[i, kind * GROUP : (kind + 1) * GROUP, :] for kind in range(3)) for i in range(SIDE)
    ]
    top, total, mixed = merge(parts)
    stat_ref[:GROUP, :] = top + jnp.log2(total)
    stat_ref[GROUP : 2 * GROUP, :] = mixed / total
    for i in range(SIDE):
        keyt_ref[i] = pair_refs[i][0].T

    q, g = load_own(q_ref, info), load_own(g_ref, info)
    keys = sk_ref[response_rows(info), :]
    log_sum, delta = (
        jnp.concatenate([own_lanes(stat_ref[first + h : first + h + 1, :], info) for h in range(GROUP)], axis=1)
        for first in (0, GROUP)
    )
    probs, dscores = score_grads(
        keys, sv_ref[response_rows(info), :], q, g, log_sum, delta, causal(info)
    )
    dself_value_ref[...] = dot_nn(probs, g)
    dself_key_ref[...] = dot_nn(dscores, q)
    dself_query_ref[...] = dot_nn(keys.T, dscores)

    for head in range(GROUP):
        log_sum = stat_ref[pl.ds(head, 1), :]
        delta = stat_ref[pl.ds(GROUP + head, 1), :]
        q, g = load_head(q_ref, head), load_head(g_ref, head)
        dq = jnp.zeros((HD, SIDE * HD), F32)
        for i in range(SIDE):
            probs, dscores = score_grads(pair_refs[i][0], pair_refs[i][1], q, g, log_sum, delta)
            dvalue, dkey = dot_nn(probs, g), dot_nn(dscores, q)
            dvalue_ref[i] = dvalue if head == 0 else dvalue_ref[i] + dvalue
            dkey_ref[i] = dkey if head == 0 else dkey_ref[i] + dkey
            dq = dq + dot_nn(keyt_ref[i], dscores)
        own = dself_query_ref[:, head_lanes(head)]
        for response in range(SIDE):
            piece = dq[:, response * HD : (response + 1) * HD]
            piece = piece + jnp.where(response == info[0], own, 0.0)
            piece_ref[response] = (piece * FACTOR).T.astype(BF16)
        for step, out_ref in zip((0,) + PLACES, (dq0_ref, dq1_ref, dq2_ref, dq3_ref)):
            response = lax.rem(info[0] + step, SIDE)
            out_ref[0, :, head_lanes(head)] = piece_ref[response]
            out_ref[1, :, head_lanes(head)] = piece_ref[response ^ 1]


def split_kernel(
    info, dkey_ref, dvalue_ref, dself_key_ref, dself_value_ref, own_ref, send1_ref, send2_ref, send3_ref
):
    for i, step, ref in zip(range(SIDE), (0,) + PLACES, (own_ref, send1_ref, send2_ref, send3_ref)):
        source = lax.rem(info[1] + SIDE - step, SIDE)
        slots = pl.ds(pl.multiple_of(source * HD, HD), HD)
        ref[:L, :HD] = (dkey_ref[i] * FACTOR).astype(ref.dtype)
        ref[:L, HD:] = dvalue_ref[i].astype(ref.dtype)
        ref[L:, :HD] = (dself_key_ref[slots, :] * FACTOR).astype(ref.dtype)
        ref[L:, HD:] = dself_value_ref[slots, :].astype(ref.dtype)


def finish_kernel(own_ref, b1_ref, b2_ref, b3_ref, dk_ref, dv_ref, dsk_ref, dsv_ref):
    total = own_ref[...] + sum(ref[...].astype(F32) for ref in (b1_ref, b2_ref, b3_ref))
    dk_ref[...] = total[:L, :HD]
    dv_ref[...] = total[:L, HD:]
    dsk_ref[...] = total[L:, :HD]
    dsv_ref[...] = total[L:, HD:]


def sum_turn_kernel(a_ref, b_ref, c_ref, d_ref, out_ref):
    total = sum(ref[...].astype(F32) for ref in (a_ref, b_ref, c_ref, d_ref))
    out_ref[...] = total.T.astype(BF16)


def project_blocks(info, weight_refs, core, rows, put):
    depth = weight_refs[0].shape[1]
    for step, weight_ref in zip((0,) + PLACES, weight_refs):
        source = lax.rem(info[1] + SIDE - step, SIDE)
        at = pl.ds(pl.multiple_of(lax.rem(source, 2) * depth, depth), depth)

        @pl.when(lax.div(source, 2) == core)
        def _():
            for block in range(2):
                terms = dot_nt(weight_ref[block], rows)
                for part in range(2):
                    put(part, block, at, terms[:, part * HD : (part + 1) * HD])


def project_theirs_kernel(
    info, d0_ref, d1_ref, d2_ref, d3_ref, w0_ref, w1_ref, w2_ref, w3_ref, out_ref, rows_ref
):
    for part in range(2):
        total = sum(ref[part].astype(F32) for ref in (d0_ref, d1_ref, d2_ref, d3_ref))
        rows_ref[part * HD : (part + 1) * HD, :] = total.astype(BF16)

    def put(part, block, at, terms):
        out_ref[part, block, at, :] = terms.astype(BF16)

    project_blocks(info, (w0_ref, w1_ref, w2_ref, w3_ref), 1 - info[2], rows_ref[...], put)


def project_mine_kernel(
    info, rows_ref, theirs_ref, w0_ref, w1_ref, w2_ref, w3_ref, o0_ref, o1_ref, o2_ref, o3_ref, out_ref
):
    columns = (info[0], SIDE - 1 - info[0])

    def put(part, block, at, terms):
        terms = terms + theirs_ref[part, block, at, :].astype(F32)
        out_ref[columns[block] ^ 1 ^ part, at, :] = terms.astype(BF16)

    project_blocks(info, (w0_ref, w1_ref, w2_ref, w3_ref), info[2], rows_ref[...], put)
    for step, ref in zip((0,) + PLACES, (o0_ref, o1_ref, o2_ref, o3_ref)):
        ref[...] = out_ref[lax.rem(info[3] + step, SIDE)]


def ring(step):
    return [(i, (i + step) % SIDE) for i in range(SIDE)]


def spread(array, axis):
    return [lax.ppermute(array, axis, ring(step)) for step in PLACES]


def body(queries, doc_keys, doc_values, self_keys, self_values, out_grads, lengths, query_weight):
    doc_rows = doc_keys.shape[0]
    place_y = lax.axis_index("y").astype(jnp.int32)
    info = jnp.stack([lax.axis_index(Z).astype(jnp.int32), place_y, lax.axis_index("core").astype(jnp.int32), lax.axis_index("x").astype(jnp.int32)])
    pair = jnp.stack([doc_keys, doc_values])
    pairs = [pair] + [lax.ppermute(pair, "y", ring(step)) for step in PLACES[:2]]
    other = lax.ppermute(query_weight, Z, [(i, SIDE - 1 - i) for i in range(SIDE)])

    def own_rows(array):
        return lax.dynamic_slice_in_dim(array.reshape(SIDE, L, WIDTH), place_y * HD, HD, 1)

    valid = (jnp.arange(HD, dtype=jnp.int32) + place_y * HD)[None, :] < lengths[:, None]
    far, valid = lax.optimization_barrier((pair, valid))
    pairs.append(lax.ppermute(far, "y", ring(PLACES[2])))
    q_own = own_rows(queries)
    g_own = own_rows(out_grads) * valid[..., None].astype(out_grads.dtype)

    smem = pl.BlockSpec(memory_space=pltpu.SMEM)
    vmem = pl.BlockSpec(memory_space=pltpu.VMEM)

    def call(kernel, shapes, operands, name, megabytes=8, scratch=()):
        return pl.pallas_call(
            kernel,
            in_specs=[smem if a is info else vmem for a in operands],
            out_specs=jax.tree.map(lambda _: vmem, shapes),
            out_shape=shapes,
            scratch_shapes=scratch,
            compiler_params=pltpu.CompilerParams(vmem_limit_bytes=megabytes * 1024 * 1024),
            name=name,
        )(*operands)

    shape = jax.ShapeDtypeStruct
    stats = call(
        own_stats_kernel,
        shape((STATS, SIDE * HD), F32),
        (info, q_own, g_own, pair, self_keys, self_values),
        "own_stats",
    )
    weight = jnp.stack([query_weight, other])
    stats = call(
        rest_stats_kernel,
        shape((STATS, SIDE * HD), F32),
        (info, q_own, g_own, *pairs[1:3], stats),
        "near_stats",
    )
    weight, stats, pairs[3] = lax.optimization_barrier((weight, stats, pairs[3]))
    weights = [weight] + spread(weight, "y")
    stats = call(
        rest_stats_kernel,
        shape((SIDE, STATS, SIDE * HD), F32),
        (info, q_own, g_own, pairs[3], stats),
        "far_stats",
    )
    parts = lax.all_to_all(stats, Z, 0, 0, tiled=True)

    grad_shape = shape((2, HD, WIDTH), BF16)
    back_shape = shape((doc_rows + HD, 2 * HD), BF16)
    found = call(
        grads_kernel,
        [grad_shape] * SIDE + [shape((SIDE, doc_rows, HD), F32)] * 2 + [shape((L, HD), F32)] * 2,
        (info, q_own, g_own, *pairs, self_keys, self_values, parts),
        "local_grads",
        megabytes=14,
        scratch=[
            pltpu.VMEM((STATS, SIDE * HD), F32),
            pltpu.VMEM((SIDE, HD, doc_rows), BF16),
            pltpu.VMEM((HD, WIDTH), F32),
            pltpu.VMEM((SIDE, HD, HD), BF16),
        ],
    )
    dq, dq_sends = found[0], found[1:SIDE]
    own, *sends = call(
        split_kernel,
        [shape(back_shape.shape, F32)] + [back_shape] * 3,
        (info, *found[SIDE:]),
        "split_grads",
    )
    dq_parts = [lax.ppermute(a, Z, ring(step)) for step, a in zip(PLACES, dq_sends)]
    weights, sends = lax.optimization_barrier((weights, sends))
    backs = [lax.ppermute(a, "y", ring(SIDE - step)) for step, a in zip(PLACES, sends)]
    columns = 2 * query_weight.shape[0]
    theirs, rows = call(
        project_theirs_kernel,
        [shape((2, 2, columns, HD), BF16), shape((2 * HD, WIDTH), BF16)],
        (info, dq, *dq_parts, *weights),
        "project_theirs",
    )
    theirs = lax.ppermute(theirs, "core", [(0, 1), (1, 0)])
    term, *terms = call(
        project_mine_kernel,
        [shape((columns, HD), BF16)] * SIDE,
        (info, rows, theirs, *weights),
        "project_mine",
        scratch=[pltpu.VMEM((SIDE, columns, HD), BF16)],
    )
    terms = [lax.ppermute(a, "x", ring(step)) for step, a in zip(PLACES, terms)]
    terms, backs[:2] = lax.optimization_barrier((terms, backs[:2]))
    input_grads = call(sum_turn_kernel, shape((HD, columns), BF16), (term, *terms), "sum_groups")
    moves = []
    for z in range(SIDE):
        for x in range(SIDE):
            partner = x in (z, SIDE - 1 - z)
            moves.append((z * SIDE + x, (z ^ 1) * SIDE + x if partner else z * SIDE + (x ^ 1)))
    input_grads = lax.ppermute(input_grads, Z + ("x",), moves)
    grads = call(
        finish_kernel,
        [shape((doc_rows, HD), F32)] * 2 + [shape((HD, HD), F32)] * 2,
        (own, *backs),
        "sum_key_values",
    )
    return (input_grads, *grads)


def solution(mesh):
    names = ("z_high", "z_low", "y", "x", "core")
    grid = Mesh(mesh.devices.reshape(2, 2, SIDE, SIDE, 2), names)
    seq, head = names[:3], names[3:]
    in_specs = (
        P(None, head),
        P(seq, head),
        P(seq, head),
        P(None, head),
        P(None, head),
        P(None, head),
        P(),
        P(seq, head),
    )
    return jax.shard_map(
        body, mesh=grid, in_specs=in_specs, out_specs=(P(seq, head),) * 5, check_vma=False
    )
```

```python
import functools
import math

import jax
import jax.numpy as jnp
from jax import lax
from jax.experimental import pallas as pl
from jax.experimental.pallas import tpu as pltpu
from jax.sharding import Mesh, PartitionSpec as P

HQ = 40
KVH = 8
HD = 128
L = 512
GROUP = HQ // KVH
WIDTH = GROUP * HD
FACTOR = HD ** (-0.5)
LOG_FACTOR = FACTOR * math.log2(math.e)
STATS = 16
SIDE = 4
LOW = -1e30
HIGH = 1e30
PLACES = (1, 3, 2)
Z = ("z_high", "z_low")
BF16 = jnp.bfloat16
F32 = jnp.float32


def dot_nt(a, b):
    return lax.dot_general(a, b, (((1,), (1,)), ((), ())), preferred_element_type=F32)


def dot_nn(a, b):
    return lax.dot_general(a, b, (((1,), (0,)), ((), ())), preferred_element_type=F32)


def head_lanes(head):
    return pl.ds(pl.multiple_of(head * HD, HD), HD)


def load_head(ref, head):
    return ref[:, :, head_lanes(head)].reshape(SIDE * HD, HD)


def load_own(ref, info):
    own = ref[info[0]]
    return jnp.concatenate([own[:, h * HD : (h + 1) * HD] for h in range(GROUP)], axis=0)


def own_lanes(row, info):
    pieces = [row[:, i * HD : (i + 1) * HD] for i in range(SIDE)]
    return sum(jnp.where(info[0] == i, piece, 0.0) for i, piece in enumerate(pieces))


def response_rows(info):
    return pl.ds(pl.multiple_of(info[0] * L, L), L)


def causal(info):
    keys = lax.broadcasted_iota(jnp.int32, (L, HD), 0)
    rows = lax.broadcasted_iota(jnp.int32, (L, HD), 1) + info[1] * HD
    return jnp.concatenate([keys <= rows] * GROUP, axis=1)


def local_stats(scores, dprods):
    top = jnp.max(scores, axis=0, keepdims=True)
    weights = jnp.exp2(scores - top)
    total = jnp.sum(weights, axis=0, keepdims=True)
    mixed = jnp.sum(weights * dprods, axis=0, keepdims=True)
    return top, total, mixed


def merge(found):
    top = functools.reduce(jnp.maximum, [item[0] for item in found])
    scales = [jnp.exp2(item[0] - top) for item in found]
    total = sum(item[1] * scale for item, scale in zip(found, scales))
    mixed = sum(item[2] * scale for item, scale in zip(found, scales))
    return top, total, mixed


def block_stats(q, g, keys, values):
    return local_stats(dot_nt(keys, q) * LOG_FACTOR, dot_nt(values, g))


def put_stats(ref, head, found):
    for kind in range(3):
        ref[pl.ds(kind * GROUP + head, 1), :] = found[kind]


def get_stats(ref, head):
    return tuple(ref[pl.ds(kind * GROUP + head, 1), :] for kind in range(3))


def own_stats_kernel(info, q_ref, g_ref, pair_ref, sk_ref, sv_ref, out_ref):
    out_ref[...] = jnp.zeros_like(out_ref)
    scores = dot_nt(sk_ref[response_rows(info), :], load_own(q_ref, info)) * LOG_FACTOR
    scores = jnp.where(causal(info), scores, -jnp.inf)
    own = local_stats(scores, dot_nt(sv_ref[response_rows(info), :], load_own(g_ref, info)))
    mine = lax.broadcasted_iota(jnp.int32, (1, SIDE * HD), 1) // HD == info[0]
    for head in range(GROUP):
        wide = [jnp.concatenate([item[:, head * HD : (head + 1) * HD]] * SIDE, axis=1) for item in own]
        put_stats(out_ref, head, [jnp.where(mine, a, b) for a, b in zip(wide, (LOW, 0.0, 0.0))])

    @pl.loop(0, GROUP, unroll=True)
    def _(head):
        found = block_stats(load_head(q_ref, head), load_head(g_ref, head), pair_ref[0], pair_ref[1])
        put_stats(out_ref, head, merge([found, get_stats(out_ref, head)]))


def rest_stats_kernel(info, q_ref, g_ref, *refs):
    pair_refs, former_ref, out_ref = refs[:-2], refs[-2], refs[-1]
    wide = len(out_ref.shape) > 2

    def put(head, found):
        for copy in range(SIDE if wide else 1):
            put_stats(out_ref.at[copy] if wide else out_ref, head, found)

    out_ref[...] = jnp.zeros_like(out_ref)

    @pl.loop(0, GROUP, unroll=True)
    def _(head):
        q, g = load_head(q_ref, head), load_head(g_ref, head)
        top, total, mixed = get_stats(former_ref, head)
        for ref in pair_refs:
            weights = jnp.exp2(dot_nt(ref[0], q) * LOG_FACTOR - top)
            total = total + jnp.sum(weights, axis=0, keepdims=True)
            mixed = mixed + jnp.sum(weights * dot_nt(ref[1], g), axis=0, keepdims=True)
        put(head, (top, total, mixed))

    sums = (out_ref.at[0] if wide else out_ref)[GROUP : 2 * GROUP, :]

    @pl.when(jnp.logical_not(jnp.max(sums) < HIGH))
    def _():
        @pl.loop(0, GROUP)
        def _(head):
            q, g = load_head(q_ref, head), load_head(g_ref, head)
            found = [get_stats(former_ref, head)]
            for ref in pair_refs:
                found.append(block_stats(q, g, ref[0], ref[1]))
            put(head, merge(found))


def score_grads(k, v, q, g, log_sum, delta, allowed=None):
    probs = jnp.exp2(dot_nt(k, q) * LOG_FACTOR - log_sum)
    if allowed is not None:
        probs = jnp.where(allowed, probs, 0.0)
    dscores = (probs * (dot_nt(v, g) - delta)).astype(BF16)
    return probs.astype(BF16), dscores


def grads_kernel(
    info, q_ref, g_ref, p0_ref, p1_ref, p2_ref, p3_ref, sk_ref, sv_ref, part_ref,
    dq0_ref, dq1_ref, dq2_ref, dq3_ref, dkey_ref, dvalue_ref, dself_key_ref, dself_value_ref,
    stat_ref, keyt_ref, dself_query_ref, piece_ref,
):
    pair_refs = (p0_ref, p1_ref, p2_ref, p3_ref)
    parts = [
        tuple(part_ref[i, kind * GROUP : (kind + 1) * GROUP, :] for kind in range(3)) for i in range(SIDE)
    ]
    top, total, mixed = merge(parts)
    stat_ref[:GROUP, :] = top + jnp.log2(total)
    stat_ref[GROUP : 2 * GROUP, :] = mixed / total
    for i in range(SIDE):
        keyt_ref[i] = pair_refs[i][0].T

    q, g = load_own(q_ref, info), load_own(g_ref, info)
    keys = sk_ref[response_rows(info), :]
    log_sum, delta = (
        jnp.concatenate([own_lanes(stat_ref[first + h : first + h + 1, :], info) for h in range(GROUP)], axis=1)
        for first in (0, GROUP)
    )
    probs, dscores = score_grads(
        keys, sv_ref[response_rows(info), :], q, g, log_sum, delta, causal(info)
    )
    dself_value_ref[...] = dot_nn(probs, g)
    dself_key_ref[...] = dot_nn(dscores, q)
    dself_query_ref[...] = dot_nn(keys.T, dscores)

    for head in range(GROUP):
        log_sum = stat_ref[pl.ds(head, 1), :]
        delta = stat_ref[pl.ds(GROUP + head, 1), :]
        q, g = load_head(q_ref, head), load_head(g_ref, head)
        dq = jnp.zeros((HD, SIDE * HD), F32)
        for i in range(SIDE):
            probs, dscores = score_grads(pair_refs[i][0], pair_refs[i][1], q, g, log_sum, delta)
            dvalue, dkey = dot_nn(probs, g), dot_nn(dscores, q)
            dvalue_ref[i] = dvalue if head == 0 else dvalue_ref[i] + dvalue
            dkey_ref[i] = dkey if head == 0 else dkey_ref[i] + dkey
            dq = dq + dot_nn(keyt_ref[i], dscores)
        own = dself_query_ref[:, head_lanes(head)]
        for response in range(SIDE):
            piece = dq[:, response * HD : (response + 1) * HD]
            piece = piece + jnp.where(response == info[0], own, 0.0)
            piece_ref[response] = (piece * FACTOR).T.astype(BF16)
        for step, out_ref in zip((0,) + PLACES, (dq0_ref, dq1_ref, dq2_ref, dq3_ref)):
            response = lax.rem(info[0] + step, SIDE)
            out_ref[0, :, head_lanes(head)] = piece_ref[response]
            out_ref[1, :, head_lanes(head)] = piece_ref[response ^ 1]


def split_kernel(
    info, dkey_ref, dvalue_ref, dself_key_ref, dself_value_ref, own_ref, send1_ref, send2_ref, send3_ref
):
    for i, step, ref in zip(range(SIDE), (0,) + PLACES, (own_ref, send1_ref, send2_ref, send3_ref)):
        source = lax.rem(info[1] + SIDE - step, SIDE)
        slots = pl.ds(pl.multiple_of(source * HD, HD), HD)
        ref[:L, :HD] = (dkey_ref[i] * FACTOR).astype(ref.dtype)
        ref[:L, HD:] = dvalue_ref[i].astype(ref.dtype)
        ref[L:, :HD] = (dself_key_ref[slots, :] * FACTOR).astype(ref.dtype)
        ref[L:, HD:] = dself_value_ref[slots, :].astype(ref.dtype)


def finish_kernel(own_ref, b1_ref, b2_ref, b3_ref, dk_ref, dv_ref, dsk_ref, dsv_ref):
    total = own_ref[...] + sum(ref[...].astype(F32) for ref in (b1_ref, b2_ref, b3_ref))
    dk_ref[...] = total[:L, :HD]
    dv_ref[...] = total[:L, HD:]
    dsk_ref[...] = total[L:, :HD]
    dsv_ref[...] = total[L:, HD:]


def sum_turn_kernel(a_ref, b_ref, c_ref, d_ref, out_ref):
    total = sum(ref[...].astype(F32) for ref in (a_ref, b_ref, c_ref, d_ref))
    out_ref[...] = total.T.astype(BF16)


def project_blocks(info, weight_refs, core, rows, put):
    depth = weight_refs[0].shape[1]
    for step, weight_ref in zip((0,) + PLACES, weight_refs):
        source = lax.rem(info[1] + SIDE - step, SIDE)
        at = pl.ds(pl.multiple_of(lax.rem(source, 2) * depth, depth), depth)

        @pl.when(lax.div(source, 2) == core)
        def _():
            for block in range(2):
                terms = dot_nt(weight_ref[block], rows)
                for part in range(2):
                    put(part, block, at, terms[:, part * HD : (part + 1) * HD])


def project_theirs_kernel(
    info, d0_ref, d1_ref, d2_ref, d3_ref, w0_ref, w1_ref, w2_ref, w3_ref, out_ref, rows_ref
):
    for part in range(2):
        total = sum(ref[part].astype(F32) for ref in (d0_ref, d1_ref, d2_ref, d3_ref))
        rows_ref[part * HD : (part + 1) * HD, :] = total.astype(BF16)

    def put(part, block, at, terms):
        out_ref[part, block, at, :] = terms.astype(BF16)

    project_blocks(info, (w0_ref, w1_ref, w2_ref, w3_ref), 1 - info[2], rows_ref[...], put)


def project_mine_kernel(
    info, rows_ref, theirs_ref, w0_ref, w1_ref, w2_ref, w3_ref, o0_ref, o1_ref, o2_ref, o3_ref, out_ref
):
    columns = (info[0], SIDE - 1 - info[0])

    def put(part, block, at, terms):
        terms = terms + theirs_ref[part, block, at, :].astype(F32)
        out_ref[columns[block] ^ 1 ^ part, at, :] = terms.astype(BF16)

    project_blocks(info, (w0_ref, w1_ref, w2_ref, w3_ref), info[2], rows_ref[...], put)
    for step, ref in zip((0,) + PLACES, (o0_ref, o1_ref, o2_ref, o3_ref)):
        ref[...] = out_ref[lax.rem(info[3] + step, SIDE)]


def ring(step):
    return [(i, (i + step) % SIDE) for i in range(SIDE)]


def spread(array, axis):
    return [lax.ppermute(array, axis, ring(step)) for step in PLACES]


def body(queries, doc_keys, doc_values, self_keys, self_values, out_grads, lengths, query_weight):
    doc_rows = doc_keys.shape[0]
    place_y = lax.axis_index("y").astype(jnp.int32)
    info = jnp.stack([lax.axis_index(Z).astype(jnp.int32), place_y, lax.axis_index("core").astype(jnp.int32), lax.axis_index("x").astype(jnp.int32)])
    pair = jnp.stack([doc_keys, doc_values])
    pairs = [pair] + [lax.ppermute(pair, "y", ring(step)) for step in PLACES[:2]]
    other = lax.ppermute(query_weight, Z, [(i, SIDE - 1 - i) for i in range(SIDE)])

    def own_rows(array):
        return lax.dynamic_slice_in_dim(array.reshape(SIDE, L, WIDTH), place_y * HD, HD, 1)

    valid = (jnp.arange(HD, dtype=jnp.int32) + place_y * HD)[None, :] < lengths[:, None]
    far, valid = lax.optimization_barrier((pair, valid))
    pairs.append(lax.ppermute(far, "y", ring(PLACES[2])))
    q_own = own_rows(queries)
    g_own = own_rows(out_grads) * valid[..., None].astype(out_grads.dtype)

    smem = pl.BlockSpec(memory_space=pltpu.SMEM)
    vmem = pl.BlockSpec(memory_space=pltpu.VMEM)

    def call(kernel, shapes, operands, name, megabytes=8, scratch=()):
        return pl.pallas_call(
            kernel,
            in_specs=[smem if a is info else vmem for a in operands],
            out_specs=jax.tree.map(lambda _: vmem, shapes),
            out_shape=shapes,
            scratch_shapes=scratch,
            compiler_params=pltpu.CompilerParams(vmem_limit_bytes=megabytes * 1024 * 1024),
            name=name,
        )(*operands)

    shape = jax.ShapeDtypeStruct
    stats = call(
        own_stats_kernel,
        shape((STATS, SIDE * HD), F32),
        (info, q_own, g_own, pair, self_keys, self_values),
        "own_stats",
    )
    weight = jnp.stack([query_weight, other])
    stats = call(
        rest_stats_kernel,
        shape((STATS, SIDE * HD), F32),
        (info, q_own, g_own, *pairs[1:3], stats),
        "near_stats",
    )
    weight, stats, pairs[3] = lax.optimization_barrier((weight, stats, pairs[3]))
    weights = [weight] + spread(weight, "y")
    stats = call(
        rest_stats_kernel,
        shape((SIDE, STATS, SIDE * HD), F32),
        (info, q_own, g_own, pairs[3], stats),
        "far_stats",
    )
    parts = lax.all_to_all(stats, Z, 0, 0, tiled=True)

    grad_shape = shape((2, HD, WIDTH), BF16)
    back_shape = shape((doc_rows + HD, 2 * HD), BF16)
    found = call(
        grads_kernel,
        [grad_shape] * SIDE + [shape((SIDE, doc_rows, HD), F32)] * 2 + [shape((L, HD), F32)] * 2,
        (info, q_own, g_own, *pairs, self_keys, self_values, parts),
        "local_grads",
        megabytes=14,
        scratch=[
            pltpu.VMEM((STATS, SIDE * HD), F32),
            pltpu.VMEM((SIDE, HD, doc_rows), BF16),
            pltpu.VMEM((HD, WIDTH), F32),
            pltpu.VMEM((SIDE, HD, HD), BF16),
        ],
    )
    dq, dq_sends = found[0], found[1:SIDE]
    own, *sends = call(
        split_kernel,
        [shape(back_shape.shape, F32)] + [back_shape] * 3,
        (info, *found[SIDE:]),
        "split_grads",
    )
    dq_parts = [lax.ppermute(a, Z, ring(step)) for step, a in zip(PLACES, dq_sends)]
    weights, sends = lax.optimization_barrier((weights, sends))
    backs = [lax.ppermute(a, "y", ring(SIDE - step)) for step, a in zip(PLACES, sends)]
    columns = 2 * query_weight.shape[0]
    theirs, rows = call(
        project_theirs_kernel,
        [shape((2, 2, columns, HD), BF16), shape((2 * HD, WIDTH), BF16)],
        (info, dq, *dq_parts, *weights),
        "project_theirs",
    )
    theirs = lax.ppermute(theirs, "core", [(0, 1), (1, 0)])
    term, *terms = call(
        project_mine_kernel,
        [shape((columns, HD), BF16)] * SIDE,
        (info, rows, theirs, *weights),
        "project_mine",
        scratch=[pltpu.VMEM((SIDE, columns, HD), BF16)],
    )
    terms = [lax.ppermute(a, "x", ring(step)) for step, a in zip(PLACES, terms)]
    terms, backs[0], backs[2] = lax.optimization_barrier((terms, backs[0], backs[2]))
    input_grads = call(sum_turn_kernel, shape((HD, columns), BF16), (term, *terms), "sum_groups")
    moves = []
    for z in range(SIDE):
        for x in range(SIDE):
            partner = x in (z, SIDE - 1 - z)
            moves.append((z * SIDE + x, (z ^ 1) * SIDE + x if partner else z * SIDE + (x ^ 1)))
    input_grads = lax.ppermute(input_grads, Z + ("x",), moves)
    grads = call(
        finish_kernel,
        [shape((doc_rows, HD), F32)] * 2 + [shape((HD, HD), F32)] * 2,
        (own, *backs),
        "sum_key_values",
    )
    return (input_grads, *grads)


def solution(mesh):
    names = ("z_high", "z_low", "y", "x", "core")
    grid = Mesh(mesh.devices.reshape(2, 2, SIDE, SIDE, 2), names)
    seq, head = names[:3], names[3:]
    in_specs = (
        P(None, head),
        P(seq, head),
        P(seq, head),
        P(None, head),
        P(None, head),
        P(None, head),
        P(),
        P(seq, head),
    )
    return jax.shard_map(
        body, mesh=grid, in_specs=in_specs, out_specs=(P(seq, head),) * 5, check_vma=False
    )
```
